128 devices in a mesh: seq: 4 (over x), fsdp: 16 (over z, y), dp: 2 (over core).
Axes of the slice: x: 4, y: 4, z: 4, core: 2. Of those that a mesh axis runs over, the one named last changes fastest.
Arguments:
- layer_input: bfloat16 [32, 1024, 8192], P(('fsdp', 'dp'), 'seq'), may hold values from -6 to 6
- c_weight: bfloat16 [8192, 512], P('fsdp'), may hold values from -0.0625 to 0.0625
- head_input: bfloat16 [32, 1024, 8192], P(('fsdp', 'dp'), 'seq'), may hold values from -6 to 6
- b_input: bfloat16 [32, 1024, 512], P(('fsdp', 'dp'), 'seq'), may hold values from -0.1796875 to 0.1796875
- log_decay: float32 [32, 64, 1024], P(('fsdp', 'dp'), None, 'seq'), may hold values from -1 to 0
- skip_gain: float32 [64], replicated, may hold values from 0.5 to 2
- out_grad: bfloat16 [32, 1024, 8192], P(('fsdp', 'dp'), 'seq'), may hold values from -0.29882812 to 0.29882812
Outputs:
- head_input_grad: bfloat16 [32, 1024, 8192], P(('fsdp', 'dp'), 'seq')
- b_input_grad: bfloat16 [32, 1024, 512], P(('fsdp', 'dp'), 'seq')
- c_weight_grad: float32 [8192, 512], P('fsdp')
- log_decay_grad: float32 [32, 64, 1024], P(('fsdp', 'dp'), None, 'seq')
- skip_gain_grad: float32 [64], replicated
The draws below stay inside these ranges and needn't reach their ends.
All inputs are finite; a program needn't handle non-finite values.
Results may differ from the reference program's by a relative error of at most 0.027.
Values may be sent and summed in bfloat16 or wider, within the bound.
A program may use at most 192 MiB of HBM per device.

```python
import math
import jax
import jax.numpy as jnp
from jax import lax

D = 8192
HEAD_COUNT = 64
P_SIZE = 128
N = 128
G = 4
BLK = 256
TOK_DEV = 256
HG = 16
DOCUMENT_COUNT = 32
DOCUMENT_TOKENS = 1024


def draw_log_decay(key, part):
    random_keys = jax.random.split(key, 7)
    fast_share = 0.5
    is_fast = jax.random.uniform(random_keys[0], (DOCUMENT_COUNT, HEAD_COUNT, 1)) < fast_share
    fast_rate = jax.random.uniform(random_keys[1], (DOCUMENT_COUNT, HEAD_COUNT, 1), minval=1.0 / 50.0, maxval=1.0 / 30.0)
    slow_rate = jax.random.uniform(random_keys[2], (DOCUMENT_COUNT, HEAD_COUNT, 1), minval=0.2, maxval=0.8) / DOCUMENT_TOKENS
    decay_speed = jnp.where(is_fast, fast_rate, slow_rate)
    span_count = DOCUMENT_TOKENS // TOK_DEV
    multiplier = jax.random.uniform(random_keys[3], (DOCUMENT_COUNT, HEAD_COUNT, span_count, 1), minval=0.5, maxval=1.5)
    multiplier = jnp.broadcast_to(multiplier, (DOCUMENT_COUNT, HEAD_COUNT, span_count, TOK_DEV)).reshape(DOCUMENT_COUNT, HEAD_COUNT, DOCUMENT_TOKENS)
    jitter_level = jax.random.uniform(random_keys[4], (DOCUMENT_COUNT, HEAD_COUNT, DOCUMENT_TOKENS), minval=0.5, maxval=1.5)
    spike_locations = jax.random.randint(random_keys[5], (DOCUMENT_COUNT, 1, 1, 2), 0, DOCUMENT_TOKENS)
    token_offsets = jnp.arange(DOCUMENT_TOKENS).reshape(1, 1, DOCUMENT_TOKENS, 1)
    spike_retained = jax.random.uniform(random_keys[6], (DOCUMENT_COUNT, HEAD_COUNT, 1, 2), minval=0.65, maxval=0.85)
    spike_values = jnp.sum(jnp.where(token_offsets == spike_locations, jnp.log(spike_retained), 0.0), axis=-1)
    return (-decay_speed * multiplier * jitter_level + spike_values).astype(jnp.float32)


def spiked(result, rng, source, target, blocks, factor):
    def block_of(position):
        return (jnp.arange(result.shape[position]) // (result.shape[position] // blocks)).reshape((-1,) + (1,) * (result.ndim - 1 - position))

    one_side = jax.random.permutation(rng, blocks)[block_of(target)]
    second = (block_of(target) + blocks // 2) % blocks
    return jnp.where((block_of(source) == one_side) | (block_of(source) == second), factor * result, result)


def levels(rng, dims, cuts, low, largest):
    level, own = 1.0, jax.random.fold_in(rng, 6)
    for position, blocks in cuts:
        steps = jnp.exp(jax.random.uniform(jax.random.fold_in(own, position), (blocks,), jnp.float32, low / len(cuts), largest / len(cuts)))
        level = level * jnp.repeat(steps, dims[position] // blocks).reshape([-1 if axis == position else 1 for axis in range(len(dims))])
    return level


def gaussian(stream_key, shape, scale, most, shards=(), kind=jnp.bfloat16):
    drawn = jax.random.normal(stream_key, shape, jnp.float32) * scale
    if len(shards) > 0:
        drawn = levels(stream_key, shape, shards, -0.22, 0.18) * drawn
    return jnp.clip(drawn, min=-most, max=most).astype(kind)


def bell_draw_with(stream_key, dims, deviation, reach, cuts, heavy, kind=jnp.bfloat16):
    entries = deviation * jax.random.normal(stream_key, dims, jnp.float32)
    if cuts:
        entries = entries * levels(stream_key, dims, cuts, -0.22, 0.18)
    return jnp.clip(spiked(entries, jax.random.fold_in(stream_key, 3), *heavy), -reach, reach).astype(kind)


def setup_inputs(seed: int = 0) -> dict:
    arg_keys = jax.random.split(jax.random.key(seed), 8)
    return {
        "layer_input": bell_draw_with(arg_keys[0], (DOCUMENT_COUNT, DOCUMENT_TOKENS, D), 1.0, 6.0, ((0, 32), (1, 4)), (0, 2, 32, 2.75)),
        "c_weight": gaussian(arg_keys[1], (D, G * N), D ** -0.5, 0.0625, ((0, 16),)),
        "head_input": gaussian(arg_keys[2], (DOCUMENT_COUNT, DOCUMENT_TOKENS, HEAD_COUNT * P_SIZE), 1.0, 6.0, ((0, 32), (1, 4))),
        "b_input": gaussian(arg_keys[3], (DOCUMENT_COUNT, DOCUMENT_TOKENS, G * N), 0.03, 0.1796875, ((0, 32), (1, 4))),
        "log_decay": draw_log_decay(jax.random.fold_in(arg_keys[7], 71), 0),
        "skip_gain": jnp.clip(jnp.exp(jax.random.uniform(arg_keys[5], (HEAD_COUNT,), jnp.float32, math.log(0.5), math.log(2.0))), 0.5, 2.0),
        "out_grad": gaussian(arg_keys[6], (DOCUMENT_COUNT, DOCUMENT_TOKENS, HEAD_COUNT * P_SIZE), 0.05, 0.29882812, ((0, 32), (1, 4))),
    }


HIGHEST = lax.Precision.HIGHEST

def block_forward(values, b_block, c_block, log_block, skip_gain, entering):
    length = values.shape[0]
    running = jnp.cumsum(log_block, axis=1)
    ending = running[:, -1]
    spread = running[:, :, None] - running[:, None, :]
    causal = jnp.arange(length)[:, None] >= jnp.arange(length)[None, :]
    decays = jnp.exp(jnp.where(causal[None], spread, -1e+30))
    b_groups = b_block.reshape(length, G, N)
    c_groups = c_block.reshape(length, G, N)
    scores = jnp.einsum('tgn,sgn->gts', c_groups, b_groups, preferred_element_type=jnp.float32)
    mixing = (decays.reshape(G, HG, length, length) * scores[:, None]).astype(jnp.bfloat16)
    grouped = values.reshape(length, G, HG, P_SIZE)
    within = jnp.einsum('gkts,sgkp->tgkp', mixing, grouped, preferred_element_type=jnp.float32)
    from_start = jnp.exp(running).T.reshape(length, G, HG, 1)
    c_decayed = c_groups[:, :, None, :].astype(jnp.float32) * from_start
    carried = jnp.einsum('tgkn,gkpn->tgkp', c_decayed, entering.reshape(G, HG, P_SIZE, N), precision=HIGHEST)
    to_end = jnp.exp(ending[None, :] - running.T).reshape(length, G, HG, 1)
    b_decayed = (b_groups[:, :, None, :].astype(jnp.float32) * to_end).astype(jnp.bfloat16)
    own_state = jnp.einsum('sgkp,sgkn->gkpn', grouped, b_decayed, preferred_element_type=jnp.float32)
    leaving = jnp.exp(ending)[:, None, None] * entering + own_state.reshape(HEAD_COUNT, P_SIZE, N)
    output = within + carried + skip_gain.reshape(G, HG)[None, :, :, None] * grouped.astype(jnp.float32)
    return (output.reshape(length, HEAD_COUNT * P_SIZE).astype(jnp.bfloat16), leaving)

def span_forward(values, b_span, c_span, log_span, skip_gain, entering):
    blocks_here = values.shape[0] // BLK
    pieces = (values.reshape(blocks_here, BLK, HEAD_COUNT * P_SIZE), b_span.reshape(blocks_here, BLK, G * N), c_span.reshape(blocks_here, BLK, G * N), jnp.moveaxis(log_span.reshape(HEAD_COUNT, blocks_here, BLK), 1, 0))

    def advance(states, block_in):
        out_block, leaving = block_forward(block_in[0], block_in[1], block_in[2], block_in[3], skip_gain, states)
        return (leaving, out_block)
    leaving, outputs = lax.scan(advance, entering, pieces)
    return (outputs.reshape(values.shape[0], HEAD_COUNT * P_SIZE), leaving)

def span_summary(values, b_span, log_span):
    length = values.shape[0]
    running = jnp.cumsum(log_span, axis=1)
    ending = running[:, -1]
    to_end = jnp.exp(ending[None, :] - running.T).reshape(length, G, HG, 1)
    b_decayed = (b_span.reshape(length, G, 1, N).astype(jnp.float32) * to_end).astype(jnp.bfloat16)
    own_state = jnp.einsum('sgkp,sgkn->gkpn', values.reshape(length, G, HG, P_SIZE), b_decayed, preferred_element_type=jnp.float32)
    return (jnp.exp(ending), own_state.reshape(HEAD_COUNT, P_SIZE, N))

def span_adjoint(grad_span, c_span, log_span):
    length = grad_span.shape[0]
    running = jnp.cumsum(log_span, axis=1)
    from_start = jnp.exp(running).T.reshape(length, G, HG, 1)
    c_decayed = (c_span.reshape(length, G, 1, N).astype(jnp.float32) * from_start).astype(jnp.bfloat16)
    adjoint = jnp.einsum('tgkp,tgkn->gkpn', grad_span.reshape(length, G, HG, P_SIZE), c_decayed, preferred_element_type=jnp.float32)
    return adjoint.reshape(HEAD_COUNT, P_SIZE, N)

def reference(layer_input, c_weight, head_input, b_input, log_decay, skip_gain, out_grad):
    weight_zero = jnp.zeros((D, G * N), jnp.float32)
    skip_zero = jnp.zeros((HEAD_COUNT,), jnp.float32)
    zero_state = jnp.zeros((HEAD_COUNT, P_SIZE, N), jnp.float32)
    spans = DOCUMENT_TOKENS // TOK_DEV

    def one_sequence(totals_in, pieces):
        input_seq, values_seq, b_seq, log_seq, grad_seq = pieces
        c_seq = jnp.dot(input_seq, c_weight, preferred_element_type=jnp.float32).astype(jnp.bfloat16)
        input_spans = input_seq.reshape(spans, TOK_DEV, D)
        value_spans = values_seq.reshape(spans, TOK_DEV, HEAD_COUNT * P_SIZE)
        b_spans = b_seq.reshape(spans, TOK_DEV, G * N)
        c_spans = c_seq.reshape(spans, TOK_DEV, G * N)
        log_spans = jnp.transpose(log_seq.reshape(HEAD_COUNT, spans, TOK_DEV), (1, 0, 2))
        grad_spans = grad_seq.reshape(spans, TOK_DEV, HEAD_COUNT * P_SIZE)
        span_decay, own_state = jax.vmap(span_summary)(value_spans, b_spans, log_spans)
        adjoint_term = jax.vmap(span_adjoint)(grad_spans, c_spans, log_spans)
        decay_low = span_decay.astype(jnp.bfloat16)
        own_low = own_state.astype(jnp.bfloat16)
        adjoint_low = adjoint_term.astype(jnp.bfloat16)

        def chain_step(running_state, link_in):
            decay_now, term_now = link_in
            updated = decay_now.astype(jnp.float32)[:, None, None] * running_state + term_now.astype(jnp.float32)
            return (updated, running_state)
        final_state, entering = lax.scan(chain_step, zero_state, (decay_low, own_low))
        first_grad, leaving_grad = lax.scan(chain_step, zero_state, (decay_low, adjoint_low), reverse=True)
        entering = lax.optimization_barrier(entering.astype(jnp.bfloat16)).astype(jnp.float32)
        leaving_grad = lax.optimization_barrier(leaving_grad.astype(jnp.bfloat16)).astype(jnp.float32)

        def one_span(span_totals, link_in):
            weight_sum, skip_tally = span_totals
            input_now, values_now, b_now, c_now, log_now, grad_now, enter_now, leave_now = link_in
            primal, pullback = jax.vjp(span_forward, values_now, b_now, c_now, log_now, skip_gain, enter_now)
            values_grad, b_grad, c_grad, log_grad, skip_part, enter_grad = pullback((grad_now, leave_now))
            weight_term = lax.dot_general(input_now, c_grad, (((0,), (0,)), ((), ())), preferred_element_type=jnp.float32)
            weight_term = lax.optimization_barrier(weight_term.astype(jnp.bfloat16)).astype(jnp.float32)
            return ((weight_sum + weight_term, skip_tally + skip_part), (values_grad, b_grad, log_grad))
        span_totals, span_grads = lax.scan(one_span, totals_in, (input_spans, value_spans, b_spans, c_spans, log_spans, grad_spans, entering, leaving_grad))
        values_grad, b_grad, log_grad = span_grads
        shaped = (values_grad.reshape(DOCUMENT_TOKENS, HEAD_COUNT * P_SIZE), b_grad.reshape(DOCUMENT_TOKENS, G * N), jnp.transpose(log_grad, (1, 0, 2)).reshape(HEAD_COUNT, DOCUMENT_TOKENS))
        return (span_totals, shaped)
    totals_out, results = lax.scan(one_sequence, (weight_zero, skip_zero), (layer_input, head_input, b_input, log_decay, out_grad))
    weight_total, skip_total = totals_out
    return (results[0], results[1], weight_total / DOCUMENT_COUNT, results[2], skip_total / DOCUMENT_COUNT)
```

```python
import jax
import jax.numpy as jnp
from jax import lax
from jax.experimental import pallas as pl
from jax.experimental.pallas import tpu as pltpu
from jax.sharding import PartitionSpec as P

HEADS = 64
GROUPS = 4
TOK = 256
HALF = 128
DIM = 8192
CH = 4
K = HEADS // CH
CW = CH * 128
OFF = 3
STEPS = 24
BF = jnp.bfloat16
F32 = jnp.float32
MESH = pl.DeviceIdType.MESH
HIGHEST = lax.Precision.HIGHEST
NT = (((1,), (1,)), ((), ()))


def dot(a, b):
    return jnp.dot(a, b, preferred_element_type=F32)


def dot_nt(a, b):
    return lax.dot_general(a, b, NT, preferred_element_type=F32)


def expand(columns):
    rows = columns.shape[0]
    return jnp.concatenate(
        [jnp.broadcast_to(columns[:, j : j + 1], (rows, 128)) for j in range(CH)], axis=1
    )


def kernel(
    li_hbm,
    cw_hbm,
    x_hbm,
    b_ref,
    log_ref,
    skip_ref,
    g_hbm,
    dx_hbm,
    db_ref,
    dw_ref,
    dlog_ref,
    dskip_ref,
    xs,
    gs,
    g3,
    x3,
    gp,
    gx2,
    li,
    w,
    er,
    own,
    lr,
    adj,
    red,
    t1,
    u1,
    t2,
    u2,
    logp,
    cum,
    fac,
    skg,
    b4,
    bt,
    cb,
    ct,
    smat,
    stmat,
    cp_own,
    cp_send,
    cp_recv,
    ds_acc,
    dc_acc,
    db_acc,
    cg,
    acc,
    xr,
    fin,
    sk,
    load_x,
    load_g,
    load_li,
    load_w,
    store_x,
    li_send,
    li_recv,
    w_send,
    w_recv,
    f_send,
    f_recv,
    b_send,
    b_recv,
    cp_ssem,
    cp_rsem,
    cg_send,
    cg_recv,
    r_send,
    r_recv,
    x_send,
    x_recv,
    a_send,
    a_recv,
    p_send,
    p_recv,
    sk_send,
    sk_recv,
):
    s = lax.axis_index("seq")
    fs = lax.axis_index("fsdp")
    c = lax.axis_index("dp")
    z, y = lax.div(fs, 4), lax.rem(fs, 4)

    def at(seq=None, zz=None, yy=None, core=None):
        seq = s if seq is None else seq
        zz = z if zz is None else zz
        yy = y if yy is None else yy
        core = c if core is None else core
        return {"seq": seq, "fsdp": zz * 4 + yy, "dp": core}

    def plus(i, n):
        return lax.rem(i + n, 4)

    def remote(src, dst, send, recv, device):
        return pltpu.make_async_remote_copy(
            src_ref=src,
            dst_ref=dst,
            send_sem=send,
            recv_sem=recv,
            device_id=device,
            device_id_type=MESH,
        )

    sibling = at(core=1 - c)

    def lanes(k):
        return pl.ds(pl.multiple_of(k * CW, CW), CW)

    def get_x(k):
        return pltpu.make_async_copy(x_hbm.at[:, lanes(k)], xs.at[k], load_x.at[k])

    def get_g(k):
        return pltpu.make_async_copy(g_hbm.at[:, lanes(k)], gs.at[k], load_g.at[k])

    def put_x(k):
        return pltpu.make_async_copy(xs.at[k], dx_hbm.at[:, lanes(k)], store_x.at[k])

    def get_w(q):
        return pltpu.make_async_copy(
            cw_hbm.at[pl.ds(pl.multiple_of(c * 256, 256), 256), pl.ds(q * 256, 256)],
            w.at[q, z, y],
            load_w.at[q],
        )

    def li_lanes(k, core):
        return pl.ds(pl.multiple_of(k * 512 + core * 256, 256), 256)

    def li_slot(slot, k):
        return li.at[slot, :, pl.ds(pl.multiple_of(k * 256, 256), 256)]

    def fwd(k):
        return remote(own.at[k], er.at[k], f_send.at[k], f_recv.at[k], at(seq=plus(s, 1)))

    def bwd(k):
        return remote(adj.at[k], lr.at[k], b_send.at[k], b_recv.at[k], at(seq=plus(s, 3)))

    def toward(axis, d):
        if axis == 0:
            return at(zz=plus(z, 1 if d == 0 else 3))
        return at(yy=plus(y, 1 if d == 0 else 3))

    def w_copy(q, p, stage, d):
        phase, second = stage // 2, stage % 2
        axis = (1 - p) if phase == 0 else p
        me = z if axis == 0 else y
        idx = me if second == 0 else plus(me, 3 if d == 0 else 1)
        rows = pl.ds(p * 128, 128) if second == 0 else pl.ds(p * 128 + d * 64, 64)
        if phase == 0:
            ref = w.at[q, idx, y, rows] if axis == 0 else w.at[q, z, idx, rows]
        else:
            ref = w.at[q, idx, :, rows] if axis == 0 else w.at[q, :, idx, rows]
        return remote(
            ref, ref, w_send.at[q, p, stage, d], w_recv.at[q, p, stage, d], toward(axis, d)
        )

    def w_start(q, stage):
        for p in range(2):
            for d in range(2):
                w_copy(q, p, stage, d).start()

    def w_wait(q, stage):
        for p in range(2):
            for d in range(2):
                w_copy(q, p, stage, d).wait_recv()

    def cp_copy(q):
        return remote(cp_send.at[q], cp_recv.at[q], cp_ssem.at[q], cp_rsem.at[q], sibling)

    def cg_copy(g):
        return remote(cg.at[0, g], cg.at[1, g], cg_send.at[g], cg_recv.at[g], sibling)

    def r_axis(p, phase):
        return p if phase == 0 else 1 - p

    def r_ref(g, p, phase, idx, rows):
        if phase == 0:
            return red.at[g, idx, :, rows] if p == 0 else red.at[g, :, idx, rows]
        return red.at[g, z, idx, rows] if p == 0 else red.at[g, idx, y, rows]

    def r_full(p):
        return pl.ds(p * 64, 64)

    def r_half(p, h):
        return pl.ds(p * 64 + h * 32, 32)

    def r_copy(g, p, stage, d):
        phase, second = stage // 2, stage % 2
        axis = r_axis(p, phase)
        me = z if axis == 0 else y
        if second == 0:
            src = r_ref(g, p, phase, plus(me, 2), r_half(p, d))
            dst = (t1 if phase == 0 else t2).at[g, p, d]
        else:
            src = r_ref(g, p, phase, plus(me, 1 if d == 0 else 3), r_full(p))
            dst = (u1 if phase == 0 else u2).at[g, p, d]
        return remote(
            src, dst, r_send.at[g, p, stage, d], r_recv.at[g, p, stage, d], toward(axis, d)
        )

    def r_start(g, stage):
        for p in range(2):
            for d in range(2):
                r_copy(g, p, stage, d).start()

    def r_middle(g, phase):
        for p in range(2):
            me = z if r_axis(p, phase) == 0 else y
            for d in range(2):
                r_copy(g, p, 2 * phase, d).wait_recv()
                ref = r_ref(g, p, phase, plus(me, 1 if d == 0 else 3), r_half(p, d))
                got = (t1 if phase == 0 else t2)[g, p, d]
                ref[...] = (ref[...].astype(F32) + got.astype(F32)).astype(BF)
                r_copy(g, p, 2 * phase + 1, d).start()

    def r_last(g, phase):
        for p in range(2):
            me = z if r_axis(p, phase) == 0 else y
            buf = u1 if phase == 0 else u2
            for d in range(2):
                r_copy(g, p, 2 * phase + 1, d).wait_recv()
            ref = r_ref(g, p, phase, me, r_full(p))
            total = ref[...].astype(F32) + buf[g, p, 0].astype(F32) + buf[g, p, 1].astype(F32)
            ref[...] = total.astype(BF)

    def x_copy(n):
        to = plus(s, n)
        return remote(red.at[to, z, y], xr.at[n - 1], x_send.at[n], x_recv.at[n], at(seq=to))

    def a_copy(n):
        to = plus(s, n)
        return remote(fin.at[c, s], fin.at[c, s], a_send.at[n], a_recv.at[n], at(seq=to))

    def p_copy():
        return remote(fin.at[c], fin.at[c], p_send, p_recv, sibling)

    def sk_copy(axis, n):
        if axis == 3:
            return remote(sk.at[3, 0], sk.at[3, 1], sk_send.at[3, 1], sk_recv.at[3, 1], sibling)
        to = (
            at(zz=plus(z, n))
            if axis == 0
            else (at(yy=plus(y, n)) if axis == 1 else at(seq=plus(s, n)))
        )
        return remote(sk.at[axis, 0], sk.at[axis, n], sk_send.at[axis, n], sk_recv.at[axis, n], to)

    def sk_range(axis):
        return range(1, 2) if axis == 3 else range(1, 4)

    get_w(0).start()
    get_w(1).start()

    def load(k, _):
        get_x(k).start()
        return _

    lax.fori_loop(0, K, load, 0)

    def load_more(k, _):
        get_g(k).start()
        return _

    lax.fori_loop(0, K, load_more, 0)

    barrier = pltpu.get_barrier_semaphore()
    peers = [sibling]
    for n in range(1, 4):
        peers += [at(seq=plus(s, n)), at(zz=plus(z, n)), at(yy=plus(y, n))]
    for peer in peers:
        pl.semaphore_signal(barrier, inc=1, device_id=peer, device_id_type=MESH)
    pl.semaphore_wait(barrier, len(peers))

    get_w(0).wait()
    w_start(0, 0)

    def load_part(k, _):
        pltpu.make_async_copy(li_hbm.at[:, li_lanes(k, c)], li_slot(0, k), load_li).start()
        remote(li_hbm.at[:, li_lanes(k, 1 - c)], li_slot(1, k), li_send, li_recv, sibling).start()
        return _

    lax.fori_loop(0, 16, load_part, 0)

    rows_i = lax.broadcasted_iota(jnp.int32, (TOK, TOK), 0)
    cols_i = lax.broadcasted_iota(jnp.int32, (TOK, TOK), 1)
    tri = jnp.where(cols_i <= rows_i, 1.0, 0.0).astype(F32)
    low = rows_i[:HALF, :HALF] >= cols_i[:HALF, :HALF]
    lane = lax.broadcasted_iota(jnp.int32, (TOK, 128), 1)
    row = lax.broadcasted_iota(jnp.int32, (TOK, 128), 0)

    logp[...] = jnp.zeros_like(logp)
    logp[:HEADS] = log_ref[...]
    running = lax.dot_general(tri, logp[...], NT, precision=HIGHEST, preferred_element_type=F32)
    cum[...] = running
    ending = running[TOK - 1 : TOK]
    middle = jnp.where(row < HALF, running[HALF // 2 - 1 : HALF // 2], running[HALF + HALF // 2 - 1 : HALF + HALF // 2])
    edge = running[HALF - 1 : HALF]
    fac[0] = jnp.exp(running)
    fac[1] = jnp.exp(ending - running)
    fac[2] = jnp.exp(running - middle)
    fac[3] = jnp.exp(middle - running)
    fac[4] = jnp.exp(jnp.where(row < HALF, edge - running, running - edge))
    skg[...] = jnp.zeros_like(skg)
    skg[0:1, :HEADS] = skip_ref[...]
    acc[...] = jnp.zeros_like(acc)
    sk[0, 0] = jnp.zeros((8, 128), F32)

    def turned(values, k):
        return pltpu.roll(values, lax.rem(128 - CH * k, 128), 1)

    def factor(n, k):
        return expand(turned(fac[n], k))

    def row_of(values, k):
        return expand(turned(values, k)[0:1])

    def decay_row(k):
        return row_of(fac[0, TOK - 8 : TOK][7:8] + jnp.zeros((8, 128), F32), k)

    for g in range(GROUPS):
        part = b_ref[:, g * 128 : (g + 1) * 128]
        b4[g] = part
        bt[g] = part.astype(F32).T.astype(BF)

    @pl.when(s == 0)
    def _():
        er[...] = jnp.zeros_like(er)

    @pl.when(s == 3)
    def _():
        lr[...] = jnp.zeros_like(lr)

    def first(k, carried):
        get_x(k).wait()
        scaled = (factor(1, k) * xs[k].astype(F32)).astype(BF)
        x3[k] = scaled
        own[k] = dot(bt[lax.div(k, CH)], scaled).astype(BF)

        @pl.when(s == 0)
        def _():
            fwd(k).start()

        return carried

    lax.fori_loop(0, K, first, 0)
    w_wait(0, 0)
    w_start(0, 1)

    def project(q):
        weights = w[q].reshape(DIM // 2, 256)
        cp_send[q] = dot(li[1], weights)
        cp_copy(q).start()
        cp_own[q] = dot(li[0], weights)

    def projected(q):
        cp_copy(q).wait_recv()
        both = (cp_own[q] + cp_recv[q]).astype(BF)
        for n in range(2):
            g = 2 * q + n
            mine = both[:, n * 128 : (n + 1) * 128]
            cb[g] = mine
            ct[g] = mine.astype(F32).T.astype(BF)
            scores = dot_nt(mine, b4[g])
            flipped = dot_nt(b4[g], mine)
            smat[g] = jnp.where(rows_i >= cols_i, scores, 0.0).astype(BF)
            stmat[g] = jnp.where(rows_i <= cols_i, flipped, 0.0).astype(BF)

    def step(i, carried):
        f = i - s

        @pl.when((f >= 0) & (f < K) & (s > 0))
        def _():
            fwd(f).wait_recv()

            @pl.when(s < 3)
            def _():
                rounded = decay_row(f).astype(BF).astype(F32)
                own[f] = (rounded * er[f].astype(F32) + own[f].astype(F32)).astype(BF)
                fwd(f).start()

        @pl.when(i == 0)
        def _():
            w_wait(0, 1)
            w_start(0, 2)
            get_w(1).wait()
            w_start(1, 0)

        @pl.when(i == 1)
        def _():
            w_wait(0, 2)
            w_start(0, 3)
            w_wait(1, 0)
            w_start(1, 1)

        @pl.when(i == 2)
        def _():
            pltpu.make_async_copy(li.at[0], li.at[0], load_li).wait()
            remote(li.at[1], li.at[1], li_send, li_recv, sibling).wait()
            w_wait(0, 3)
            project(0)

        @pl.when(i == 3)
        def _():
            projected(0)
            w_wait(1, 1)
            w_start(1, 2)

        @pl.when(i == 4)
        def _():
            w_wait(1, 2)
            w_start(1, 3)

        @pl.when(i == 6)
        def _():
            w_wait(1, 3)
            project(1)

        @pl.when(i == 7)
        def _():
            projected(1)

        b = i - (3 - s) - OFF
        bg = lax.div(b, CH)
        active = (b >= 0) & (b < K)

        @pl.when(active & (s > 0))
        def _():
            adj[b] = dot(ct[bg], g3[b]).astype(BF)

        @pl.when(active & (s < 3))
        def _():
            bwd_wait(b)

            @pl.when(s > 0)
            def _():
                rounded = decay_row(b).astype(BF).astype(F32)
                adj[b] = (rounded * lr[b].astype(F32) + adj[b].astype(F32)).astype(BF)

        @pl.when(active & (s > 0))
        def _():
            bwd(b).start()

        @pl.when(i < K)
        def _():
            prepare(i)

        @pl.when((f >= 0) & (f < K))
        def _():
            carry(f)

        r = i - s - CH
        rg, rs = lax.div(r, CH), lax.rem(r, CH)

        @pl.when((r >= CH) & (rs == 0) & (rg <= GROUPS))
        def _():
            r_last(rg - 1, 1)

        @pl.when((r >= 0) & (rg < GROUPS))
        def _():
            @pl.when(rs == 0)
            def _():
                weight_term(rg)
                r_start(rg, 0)

            @pl.when(rs == 1)
            def _():
                r_middle(rg, 0)

            @pl.when(rs == 2)
            def _():
                r_last(rg, 0)
                r_start(rg, 2)

            @pl.when(rs == 3)
            def _():
                r_middle(rg, 1)

        @pl.when(active)
        def _():
            finish(b)

        for axis in range(4):

            @pl.when(i == K + axis)
            def _():
                if axis > 0:
                    skip_sum(axis - 1)
                for n in sk_range(axis):
                    sk_copy(axis, n).start()

        return carried

    def bwd_wait(b):
        bwd(b).wait_recv()

    def skip_sum(axis):
        total = sk[axis, 0]
        for n in sk_range(axis):
            sk_copy(axis, n).wait_recv()
            total = total + sk[axis, n]
        if axis < 3:
            sk[axis + 1, 0] = total
        else:
            dskip_ref[...] = total[0:1, :HEADS] * (1.0 / 32.0)

    def prepare(k):
        g = lax.div(k, CH)
        get_g(k).wait()
        xv = xs[k].astype(F32)
        gv = gs[k].astype(F32)
        g3[k] = (factor(0, k) * gv).astype(BF)
        gpv = (factor(2, k) * gv).astype(BF)
        xpv = (factor(3, k) * xv).astype(BF)
        cross = factor(4, k)
        x2 = (cross[:HALF] * xv[:HALF]).astype(BF)
        g2 = (cross[HALF:] * gv[HALF:]).astype(BF)
        gp[k] = gpv
        gx2[k, :HALF] = x2
        gx2[k, HALF:] = g2
        product = jnp.sum(gv * xv, axis=0, keepdims=True)
        lane8 = lane[:8]
        tally = sk[0, 0]
        for j in range(CH):
            one = jnp.sum(product[:, j * 128 : (j + 1) * 128], axis=1, keepdims=True)
            tally = jnp.where(lane8 == CH * k + j, one, tally)
        sk[0, 0] = tally
        xs[k] = xpv
        fresh = lax.rem(k, CH) == 0
        for n, (left, right) in enumerate(((gpv[:HALF], xpv[:HALF]), (g2, x2), (gpv[HALF:], xpv[HALF:]))):
            more = dot_nt(left, right)
            ds_acc[g, n] = jnp.where(fresh, 0.0, ds_acc[g, n]) + more

    def blocks_of(g):
        return (
            jnp.where(low, ds_acc[g, 0], 0.0).astype(BF),
            ds_acc[g, 1].astype(BF),
            jnp.where(low, ds_acc[g, 2], 0.0).astype(BF),
        )

    def carry(f):
        g = lax.div(f, CH)
        fresh = lax.rem(f, CH) == 0
        dc_acc[...] = jnp.where(fresh, 0.0, dc_acc[...]) + dot_nt(g3[f], er[f])

        @pl.when(lax.rem(f, CH) == CH - 1)
        def _():
            d00, d10, d11 = blocks_of(g)
            b0, b1 = b4[g, :HALF], b4[g, HALF:]
            cg[0, g, :HALF] = (dc_acc[:HALF] + dot(d00, b0)).astype(BF)
            cg[0, g, HALF:] = (dc_acc[HALF:] + dot(d10, b0) + dot(d11, b1)).astype(BF)
            cg_copy(g).start()

    def weight_term(g):
        cg_copy(g).wait_recv()
        mine = cg[0, g].astype(F32).T.astype(BF)
        other = cg[1, g].astype(F32).T.astype(BF)
        for n in range(16):
            part = slice(n * 256, (n + 1) * 256)
            term = dot(mine, li[0, :, part]) + dot(other, li[1, :, part])
            red[g, n // 4, n % 4] = term.astype(BF)

    def finish(k):
        g = lax.div(k, CH)
        sm, st = smat[g], stmat[g]
        gpv, xpv, cross = gp[k], xs[k], gx2[k]
        g3v, x3v, ev, lv = g3[k], x3[k], er[k], lr[k]
        y0 = dot(sm[:HALF, :HALF], xpv[:HALF])
        y1 = dot(sm[HALF:, HALF:], xpv[HALF:])
        yo = dot(sm[HALF:, :HALF], cross[:HALF])
        d0 = dot(st[:HALF, :HALF], gpv[:HALF])
        d1 = dot(st[HALF:, HALF:], gpv[HALF:])
        do = dot(st[:HALF, HALF:], cross[HALF:])
        yc = dot(cb[g], ev)
        zv = dot(b4[g], lv)
        cross32, gp32, xp32 = cross.astype(F32), gpv.astype(F32), xpv.astype(F32)
        zc = x3v.astype(F32) * zv
        v = g3v.astype(F32) * yc - zc
        v0 = v[:HALF] + gp32[:HALF] * y0 - xp32[:HALF] * d0 - cross32[:HALF] * do
        v1 = v[HALF:] + gp32[HALF:] * y1 - xp32[HALF:] * d1 + cross32[HALF:] * yo
        f3, f4 = factor(3, k), factor(4, k)
        direct = row_of(skg[...], k) * gs[k].astype(F32) + factor(1, k) * zv
        dx0 = direct[:HALF] + f3[:HALF] * d0 + f4[:HALF] * do
        dx1 = direct[HALF:] + f3[HALF:] * d1
        xs[k, :HALF] = dx0.astype(BF)
        xs[k, HALF:] = dx1.astype(BF)
        put_x(k).start()
        through = jnp.sum(ev.astype(F32) * lv.astype(F32), axis=0, keepdims=True)
        total = decay_row(k) * through + jnp.sum(zc, axis=0, keepdims=True)
        tally = acc[...]
        for j in range(CH):
            part = slice(j * 128, (j + 1) * 128)
            r0 = jnp.sum(v0[:, part], axis=1, keepdims=True)
            r1 = jnp.sum(v1[:, part], axis=1, keepdims=True)
            one = jnp.sum(total[:, part], axis=1, keepdims=True)
            column = jnp.concatenate([r0, r1], axis=0) + jnp.where(row == TOK - 1, one, 0.0)
            tally = jnp.where(lane == CH * k + j, column, tally)
        acc[...] = tally
        fresh = lax.rem(k, CH) == 0
        db_acc[...] = jnp.where(fresh, 0.0, db_acc[...]) + dot_nt(x3v, lv)

        @pl.when(lax.rem(k, CH) == CH - 1)
        def _():
            d00, d10, d11 = (d.astype(F32).T.astype(BF) for d in blocks_of(g))
            c0, c1 = cb[g, :HALF], cb[g, HALF:]
            there = pl.ds(pl.multiple_of(g * 128, 128), 128)
            db_ref[:HALF, there] = (db_acc[:HALF] + dot(d00, c0) + dot(d10, c1)).astype(BF)
            db_ref[HALF:, there] = (db_acc[HALF:] + dot(d11, c1)).astype(BF)

    lax.fori_loop(0, STEPS, step, 0)
    skip_sum(3)

    for n in range(1, 4):
        x_copy(n).start()
    turned_acc = acc[...].T
    dlog = jnp.dot(turned_acc, tri, precision=HIGHEST, preferred_element_type=F32)
    dlog_ref[...] = dlog[:HEADS]
    total = red[s, z, y].astype(F32)
    for n in range(1, 4):
        x_copy(n).wait_recv()
    for n in range(3):
        total = total + xr[n].astype(F32)
    fin[c, s] = total.astype(BF)
    for n in range(1, 4):
        a_copy(n).start()
    for n in range(1, 4):
        a_copy(n).wait_recv()
    p_copy().start()
    p_copy().wait_recv()
    for h in range(2):
        for g in range(GROUPS):
            dw_ref[h * 256 : (h + 1) * 256, g * 128 : (g + 1) * 128] = fin[h, g].astype(F32).T * (
                1.0 / 32.0
            )

    def drain(k, carried):
        put_x(k).wait()

        @pl.when(s < 3)
        def _():
            fwd(k).wait_send()

        @pl.when(s > 0)
        def _():
            bwd(k).wait_send()

        return carried

    lax.fori_loop(0, K, drain, 0)

    def drain_groups(g, _):
        cg_copy(g).wait_send()
        for p in range(2):
            for stage in range(4):
                for d in range(2):
                    r_copy(g, p, stage, d).wait_send()
        return _

    lax.fori_loop(0, GROUPS, drain_groups, 0)
    for q in range(2):
        cp_copy(q).wait_send()
        for p in range(2):
            for stage in range(4):
                for d in range(2):
                    w_copy(q, p, stage, d).wait_send()
    for n in range(1, 4):
        x_copy(n).wait_send()
        a_copy(n).wait_send()
    p_copy().wait_send()
    for axis in range(4):
        for n in sk_range(axis):
            sk_copy(axis, n).wait_send()


def on_device(layer_input, c_weight, head_input, b_input, log_decay, skip_gain, out_grad):
    vmem = pl.BlockSpec(memory_space=pltpu.VMEM)
    hbm = pl.BlockSpec(memory_space=pl.ANY)
    dma = pltpu.SemaphoreType.DMA

    def bf(*shape):
        return pltpu.VMEM(shape, BF)

    def f32(*shape):
        return pltpu.VMEM(shape, F32)

    chunked = (K, TOK, CW)
    states = (K, 128, CW)
    dx, db, dw, dlog, dskip = pl.pallas_call(
        kernel,
        out_shape=(
            jax.ShapeDtypeStruct((TOK, DIM), BF),
            jax.ShapeDtypeStruct((TOK, 512), BF),
            jax.ShapeDtypeStruct((512, 512), F32),
            jax.ShapeDtypeStruct((HEADS, TOK), F32),
            jax.ShapeDtypeStruct((1, HEADS), F32),
        ),
        in_specs=[hbm, hbm, hbm, vmem, vmem, vmem, hbm],
        out_specs=(hbm, vmem, vmem, vmem, vmem),
        scratch_shapes=[
            bf(*chunked),
            bf(*chunked),
            bf(*chunked),
            bf(*chunked),
            bf(*chunked),
            bf(*chunked),
            bf(2, TOK, DIM // 2),
            bf(2, 4, 4, 256, 256),
            bf(*states),
            bf(*states),
            bf(*states),
            bf(*states),
            bf(GROUPS, 4, 4, 128, 256),
            bf(GROUPS, 2, 2, 4, 32, 256),
            bf(GROUPS, 2, 2, 4, 64, 256),
            bf(GROUPS, 2, 2, 32, 256),
            bf(GROUPS, 2, 2, 64, 256),
            f32(128, TOK),
            f32(TOK, 128),
            f32(5, TOK, 128),
            f32(8, 128),
            bf(GROUPS, TOK, 128),
            bf(GROUPS, 128, TOK),
            bf(GROUPS, TOK, 128),
            bf(GROUPS, 128, TOK),
            bf(GROUPS, TOK, TOK),
            bf(GROUPS, TOK, TOK),
            f32(2, TOK, 256),
            f32(2, TOK, 256),
            f32(2, TOK, 256),
            f32(GROUPS, 3, HALF, HALF),
            f32(TOK, 128),
            f32(TOK, 128),
            bf(2, GROUPS, TOK, 128),
            f32(TOK, 128),
            bf(3, 128, 256),
            bf(2, GROUPS, 128, 256),
            f32(4, 4, 8, 128),
            dma((K,)),
            dma((K,)),
            dma,
            dma((2,)),
            dma((K,)),
            dma,
            dma,
            dma((2, 2, 4, 2)),
            dma((2, 2, 4, 2)),
            dma((K,)),
            dma((K,)),
            dma((K,)),
            dma((K,)),
            dma((2,)),
            dma((2,)),
            dma((GROUPS,)),
            dma((GROUPS,)),
            dma((GROUPS, 2, 4, 2)),
            dma((GROUPS, 2, 4, 2)),
            dma((4,)),
            dma((4,)),
            dma((4,)),
            dma((4,)),
            dma,
            dma,
            dma((4, 4)),
            dma((4, 4)),
        ],
        compiler_params=pltpu.CompilerParams(
            collective_id=0, has_side_effects=True, vmem_limit_bytes=62 * 1024 * 1024
        ),
    )(
        layer_input[0],
        c_weight,
        head_input[0],
        b_input[0],
        log_decay[0],
        skip_gain[None],
        out_grad[0],
    )
    return dx[None], db[None], dw, dlog[None], dskip[0]


def solution(mesh):
    token = P(("fsdp", "dp"), "seq", None)
    decay = P(("fsdp", "dp"), None, "seq")
    rows = P("fsdp", None)
    return jax.shard_map(
        on_device,
        mesh=mesh,
        in_specs=(token, rows, token, token, decay, P(), token),
        out_specs=(token, token, rows, decay, P()),
        check_vma=False,
    )
```

```python
import jax
import jax.numpy as jnp
from jax import lax
from jax.experimental import pallas as pl
from jax.experimental.pallas import tpu as pltpu
from jax.sharding import PartitionSpec as P

HEADS = 64
GROUPS = 4
TOK = 256
HALF = 128
DIM = 8192
CH = 4
K = HEADS // CH
CW = CH * 128
AHEAD = 4
STEPS = 28
BF = jnp.bfloat16
F32 = jnp.float32
MESH = pl.DeviceIdType.MESH
HIGHEST = lax.Precision.HIGHEST
NT = (((1,), (1,)), ((), ()))


def dot(a, b):
    return jnp.dot(a, b, preferred_element_type=F32)


def dot_nt(a, b):
    return lax.dot_general(a, b, NT, preferred_element_type=F32)


def kernel(
    li_hbm,
    cw_hbm,
    x_hbm,
    b_ref,
    log_ref,
    skip_ref,
    g_hbm,
    dx_hbm,
    db_ref,
    fin,
    dlog_ref,
    dskip_ref,
    xs,
    gs,
    gb,
    xb,
    li,
    w,
    er,
    own,
    eout,
    lr,
    adj,
    red,
    t1,
    u1,
    t2,
    u2,
    ft,
    ft2,
    vals,
    b4,
    bt,
    cb,
    ct,
    ls,
    ly,
    s10,
    cp_own,
    cp_send,
    cp_recv,
    ds_acc,
    dc_acc,
    db_acc,
    cg,
    acc,
    xr,
    sk,
    load_x,
    load_g,
    load_li,
    load_w,
    store_x,
    li_send,
    li_recv,
    w_send,
    w_recv,
    f_send,
    f_recv,
    b_send,
    b_recv,
    cp_ssem,
    cp_rsem,
    cg_send,
    cg_recv,
    r_send,
    r_recv,
    x_send,
    x_recv,
    a_send,
    a_recv,
    sk_send,
    sk_recv,
):
    s = lax.axis_index("seq")
    fs = lax.axis_index("fsdp")
    c = lax.axis_index("dp")
    z, y = lax.div(fs, 4), lax.rem(fs, 4)

    def at(seq=None, zz=None, yy=None, core=None):
        seq = s if seq is None else seq
        zz = z if zz is None else zz
        yy = y if yy is None else yy
        core = c if core is None else core
        return {"seq": seq, "fsdp": zz * 4 + yy, "dp": core}

    def plus(i, n):
        return lax.rem(i + n, 4)

    def remote(src, dst, send, recv, device):
        return pltpu.make_async_remote_copy(
            src_ref=src,
            dst_ref=dst,
            send_sem=send,
            recv_sem=recv,
            device_id=device,
            device_id_type=MESH,
        )

    sibling = at(core=1 - c)

    def lanes(k):
        return pl.ds(pl.multiple_of(k * CW, CW), CW)

    def get_x(k):
        return pltpu.make_async_copy(x_hbm.at[:, lanes(k)], xs.at[k], load_x.at[k])

    def get_g(k):
        return pltpu.make_async_copy(g_hbm.at[:, lanes(k)], gs.at[k], load_g.at[k])

    def put_x(k):
        return pltpu.make_async_copy(gs.at[k], dx_hbm.at[:, lanes(k)], store_x.at[k])

    def get_w(q):
        return pltpu.make_async_copy(
            cw_hbm.at[pl.ds(pl.multiple_of(c * 256, 256), 256), pl.ds(q * 128, 128)],
            w.at[q, z, y],
            load_w.at[q],
        )

    def li_lanes(k, core):
        return pl.ds(pl.multiple_of(k * 512 + core * 256, 256), 256)

    def li_slot(slot, k):
        return li.at[slot, :, pl.ds(pl.multiple_of(k * 256, 256), 256)]

    def fwd(k):
        return remote(eout.at[k], er.at[k], f_send.at[k], f_recv.at[k], at(seq=plus(s, 1)))

    def bwd(k):
        return remote(adj.at[k], lr.at[k], b_send.at[k], b_recv.at[k], at(seq=plus(s, 3)))

    def toward(axis, d):
        if axis == 0:
            return at(zz=plus(z, 1 if d == 0 else 3))
        return at(yy=plus(y, 1 if d == 0 else 3))

    def w_copy(q, p, stage, d):
        phase, second = stage // 2, stage % 2
        axis = (1 - p) if phase == 0 else p
        me = z if axis == 0 else y
        idx = me if second == 0 else plus(me, 3 if d == 0 else 1)
        rows = pl.ds(p * 128, 128) if second == 0 else pl.ds(p * 128 + d * 64, 64)
        if phase == 0:
            ref = w.at[q, idx, y, rows] if axis == 0 else w.at[q, z, idx, rows]
        else:
            ref = w.at[q, idx, :, rows] if axis == 0 else w.at[q, :, idx, rows]
        return remote(
            ref, ref, w_send.at[q, p, stage, d], w_recv.at[q, p, stage, d], toward(axis, d)
        )

    def w_start(q, stage):
        for p in range(2):
            for d in range(2):
                w_copy(q, p, stage, d).start()

    def w_wait(q, stage):
        for p in range(2):
            for d in range(2):
                w_copy(q, p, stage, d).wait_recv()

    def cp_copy(q):
        return remote(cp_send.at[q], cp_recv.at[q], cp_ssem.at[q], cp_rsem.at[q], sibling)

    def cg_copy(g):
        return remote(cg.at[0, g], cg.at[1, g], cg_send.at[g], cg_recv.at[g], sibling)

    def r_axis(p, phase):
        return p if phase == 0 else 1 - p

    def r_ref(g, p, phase, idx, rows):
        if phase == 0:
            return red.at[g, idx, :, rows] if p == 0 else red.at[g, :, idx, rows]
        return red.at[g, z, idx, rows] if p == 0 else red.at[g, idx, y, rows]

    def r_full(p):
        return pl.ds(p * 64, 64)

    def r_half(p, h):
        return pl.ds(p * 64 + h * 32, 32)

    def r_copy(g, p, stage, d):
        phase, second = stage // 2, stage % 2
        axis = r_axis(p, phase)
        me = z if axis == 0 else y
        if second == 0:
            src = r_ref(g, p, phase, plus(me, 2), r_half(p, d))
            dst = (t1 if phase == 0 else t2).at[g, p, d]
        else:
            src = r_ref(g, p, phase, plus(me, 1 if d == 0 else 3), r_full(p))
            dst = (u1 if phase == 0 else u2).at[g, p, d]
        return remote(
            src, dst, r_send.at[g, p, stage, d], r_recv.at[g, p, stage, d], toward(axis, d)
        )

    def r_start(g, stage):
        for p in range(2):
            for d in range(2):
                r_copy(g, p, stage, d).start()

    def r_middle(g, phase):
        for p in range(2):
            me = z if r_axis(p, phase) == 0 else y
            for d in range(2):
                r_copy(g, p, 2 * phase, d).wait_recv()
                ref = r_ref(g, p, phase, plus(me, 1 if d == 0 else 3), r_half(p, d))
                got = (t1 if phase == 0 else t2)[g, p, d]
                ref[...] = (ref[...].astype(F32) + got.astype(F32)).astype(BF)
                r_copy(g, p, 2 * phase + 1, d).start()

    def r_last(g, phase):
        for p in range(2):
            me = z if r_axis(p, phase) == 0 else y
            buf = u1 if phase == 0 else u2
            for d in range(2):
                r_copy(g, p, 2 * phase + 1, d).wait_recv()
            ref = r_ref(g, p, phase, me, r_full(p))
            total = ref[...].astype(F32) + buf[g, p, 0].astype(F32) + buf[g, p, 1].astype(F32)
            ref[...] = total.astype(BF)

    def x_copy(n):
        to = plus(s, n)
        return remote(red.at[to, z, y], xr.at[n - 1], x_send.at[n], x_recv.at[n], at(seq=to))

    def a_copy(n, other):
        to = at(seq=plus(s, n), core=1 - c if other else c)
        return remote(fin.at[c, s], fin.at[c, s], a_send.at[n, other], a_recv.at[n, other], to)

    spread = [(n, other) for other in range(2) for n in range(4)][1:]

    def sk_copy(axis, n):
        if axis == 3:
            return remote(sk.at[3, 0], sk.at[3, 1], sk_send.at[3, 1], sk_recv.at[3, 1], sibling)
        to = (
            at(zz=plus(z, n))
            if axis == 0
            else (at(yy=plus(y, n)) if axis == 1 else at(seq=plus(s, n)))
        )
        return remote(sk.at[axis, 0], sk.at[axis, n], sk_send.at[axis, n], sk_recv.at[axis, n], to)

    def sk_range(axis):
        return range(1, 2) if axis == 3 else range(1, 4)

    for q in range(4):
        get_w(q).start()

    def load(k, carried):
        get_x(k).start()
        return carried

    lax.fori_loop(0, K, load, 0)

    barrier = pltpu.get_barrier_semaphore()
    peers = [sibling]
    for n in range(1, 4):
        peers += [at(seq=plus(s, n)), at(zz=plus(z, n)), at(yy=plus(y, n))]
        peers += [at(seq=plus(s, n), core=1 - c)]
    for peer in peers:
        pl.semaphore_signal(barrier, inc=1, device_id=peer, device_id_type=MESH)

    def load_more(k, carried):
        get_g(k).start()
        return carried

    lax.fori_loop(0, K, load_more, 0)

    rows_i = lax.broadcasted_iota(jnp.int32, (TOK, TOK), 0)
    cols_i = lax.broadcasted_iota(jnp.int32, (TOK, TOK), 1)
    tri = jnp.where(cols_i <= rows_i, 1.0, 0.0).astype(F32)
    low = rows_i[:HALF, :HALF] >= cols_i[:HALF, :HALF]
    high = rows_i[:HALF, :HALF] <= cols_i[:HALF, :HALF]
    lane = lax.broadcasted_iota(jnp.int32, (TOK, 128), 1)
    row = lax.broadcasted_iota(jnp.int32, (TOK, 128), 0)
    row128 = lax.broadcasted_iota(jnp.int32, (HALF, 1), 0)
    picks = jnp.where(
        lax.rem(lax.broadcasted_iota(jnp.int32, (2 * CH, CW), 0), CH)
        == lax.div(lax.broadcasted_iota(jnp.int32, (2 * CH, CW), 1), 128),
        1.0,
        0.0,
    ).astype(BF)

    running = lax.dot_general(log_ref[...], tri, NT, precision=HIGHEST, preferred_element_type=F32)
    ending = running[:, TOK - 1 : TOK]
    mid0 = running[:, HALF // 2 - 1 : HALF // 2]
    mid1 = running[:, HALF + HALF // 2 - 1 : HALF + HALF // 2]
    for n, value in enumerate((ending, ending - mid0, ending - mid1, mid0, mid1)):
        vals[n] = jnp.broadcast_to(jnp.exp(value), (HEADS, 128))
    gain = jnp.concatenate([skip_ref[...]] * 2, axis=1)
    gains = jnp.where(lane[:HEADS] == row[:HEADS], gain, 0.0)
    vals[5] = jnp.broadcast_to(jnp.sum(gains, axis=1, keepdims=True), (HEADS, 128))
    middle = jnp.where(cols_i[:HEADS] < HALF, mid0, mid1)

    def split(values):
        coarse = values.astype(BF).astype(F32)
        return coarse, (values - coarse).astype(BF).astype(F32)

    for n, values in enumerate((running - middle, middle - running)):
        for half, part in enumerate(split(jnp.exp(values))):
            for k in range(K):
                ft[n, k, half * CH : (half + 1) * CH] = part[k * CH : (k + 1) * CH]
    for half, part in enumerate(split(jnp.exp(running[:, HALF:] - mid0))):
        for k in range(K):
            ft2[k, half * CH : (half + 1) * CH] = part[k * CH : (k + 1) * CH]
    acc[...] = jnp.zeros_like(acc)
    sk[0, 0] = jnp.zeros((8, 128), F32)

    def factor(n, k):
        return dot(ft[n, k].T.astype(BF), picks)

    def row_of(n, k):
        return jnp.concatenate([vals[n, pl.ds(CH * k + j, 1), :] for j in range(CH)], axis=1)

    for g in range(GROUPS):
        part = b_ref[:, g * 128 : (g + 1) * 128]
        b4[g] = part
        bt[g] = part.astype(F32).T.astype(BF)
        ls[g, :HALF, 256:] = part[:HALF]
        ls[g, HALF:, 128:256] = part[HALF:]

    @pl.when(s == 0)
    def _():
        er[...] = jnp.zeros_like(er)

    @pl.when(s == 3)
    def _():
        lr[...] = jnp.zeros_like(lr)
        own[...] = jnp.zeros_like(own)

    def first(k):
        g = lax.div(k, CH)
        get_x(k).wait()
        scaled = (factor(1, k) * xs[k].astype(F32)).astype(BF)
        xb[k, :128] = scaled[:HALF]
        xb[k, 256:384] = scaled[HALF:]

        @pl.when(s < 3)
        def _():
            state = row_of(1, k) * dot(bt[g, :, :HALF], scaled[:HALF])
            state = (state + row_of(2, k) * dot(bt[g, :, HALF:], scaled[HALF:])).astype(BF)
            own[k] = state

            @pl.when(s == 0)
            def _():
                eout[k] = state
                fwd(k).start()

    pl.semaphore_wait(barrier, len(peers))
    for q in range(4):
        get_w(q).wait()
        w_start(q, 0)

    def load_part(k, carried):
        pltpu.make_async_copy(li_hbm.at[:, li_lanes(k, c)], li_slot(0, k), load_li).start()
        remote(li_hbm.at[:, li_lanes(k, 1 - c)], li_slot(1, k), li_send, li_recv, sibling).start()
        return carried

    lax.fori_loop(0, 16, load_part, 0)

    def first_of(k, carried):
        first(k)
        return carried

    lax.fori_loop(0, AHEAD, first_of, 0)
    for q in range(4):
        w_wait(q, 0)
        w_start(q, 1)
    w_wait(0, 1)
    w_start(0, 2)

    pairs = lax.div(s * (s - 1), 2)
    triples = lax.div(s * (s - 1) * (s - 2), 6)
    slot_a = 1 + 2 * s - 3 * pairs + 2 * triples
    slot_b = 3 + 2 * s - 3 * pairs + triples
    slot_c = 5 + s - pairs - 3 * triples
    slot_d = slot_c + 2
    slot_e = slot_c + 4
    trail = 9 - s - pairs - triples

    def project(q):
        weights = w[q].reshape(DIM // 2, 128)
        cp_send[q] = dot(li[1], weights)
        cp_copy(q).start()
        cp_own[q] = dot(li[0], weights)

    def projected(g):
        cp_copy(g).wait_recv()
        mine = (cp_own[g] + cp_recv[g]).astype(BF)
        cb[g] = mine
        ct[g] = mine.astype(F32).T.astype(BF)
        scores = dot_nt(mine, b4[g])
        flipped = dot_nt(b4[g], mine)
        ly[g, :HALF, :128] = jnp.where(low, scores[:HALF, :HALF], 0.0).astype(BF)
        ly[g, HALF:, :128] = jnp.where(low, scores[HALF:, HALF:], 0.0).astype(BF)
        ly[g, :, 128:] = mine
        s10[g] = scores[HALF:, :HALF].astype(BF)
        ls[g, :HALF, :128] = jnp.where(high, flipped[:HALF, :HALF], 0.0).astype(BF)
        ls[g, :HALF, 128:256] = flipped[:HALF, HALF:].astype(BF)
        ls[g, HALF:, :128] = jnp.where(high, flipped[HALF:, HALF:], 0.0).astype(BF)

    def step(i, carried):
        f = i - s

        @pl.when((f >= 0) & (f < K) & (s > 0))
        def _():
            fwd(f).wait_recv()

            @pl.when(s < 3)
            def _():
                rounded = row_of(0, f).astype(BF).astype(F32)
                eout[f] = (rounded * er[f].astype(F32) + own[f].astype(F32)).astype(BF)
                fwd(f).start()

        @pl.when(i + AHEAD < K)
        def _():
            first(i + AHEAD)

        for g, slot in enumerate((slot_b, slot_c, slot_d, slot_e)):

            @pl.when(i == slot + 1)
            def _():
                projected(g)

        b = i - trail

        @pl.when((b >= 0) & (b < K))
        def _():
            bg = lax.div(b, CH)

            @pl.when(s > 0)
            def _():
                term = row_of(3, b) * dot(ct[bg, :, :HALF], gb[b, :128])
                term = term + row_of(4, b) * dot(ct[bg, :, HALF:], gb[b, 384:512])
                adj[b] = term.astype(BF)

            @pl.when(s < 3)
            def _():
                bwd(b).wait_recv()

                @pl.when(s > 0)
                def _():
                    rounded = row_of(0, b).astype(BF).astype(F32)
                    adj[b] = (rounded * lr[b].astype(F32) + adj[b].astype(F32)).astype(BF)

            @pl.when(s > 0)
            def _():
                bwd(b).start()

        @pl.when(i == slot_a)
        def _():
            w_wait(0, 2)
            w_start(0, 3)
            w_wait(1, 1)
            w_start(1, 2)

        @pl.when(i == slot_b)
        def _():
            pltpu.make_async_copy(li.at[0], li.at[0], load_li).wait()
            remote(li.at[1], li.at[1], li_send, li_recv, sibling).wait()
            w_wait(0, 3)
            project(0)
            w_wait(1, 2)
            w_start(1, 3)
            w_wait(2, 1)
            w_start(2, 2)

        @pl.when(i == slot_c)
        def _():
            w_wait(1, 3)
            project(1)
            w_wait(2, 2)
            w_start(2, 3)
            w_wait(3, 1)
            w_start(3, 2)

        @pl.when(i == slot_d)
        def _():
            w_wait(2, 3)
            project(2)
            w_wait(3, 2)
            w_start(3, 3)

        @pl.when(i == slot_e)
        def _():
            w_wait(3, 3)
            project(3)

        @pl.when(i < K)
        def _():
            prepare(i)

        @pl.when((f >= 0) & (f < K))
        def _():
            carry(f)

        @pl.when((b >= 1) & (b <= K))
        def _():
            finish(b - 1)

        for stage in range(5):
            r = f - CH - 2 * stage

            @pl.when((r >= 0) & (r < GROUPS * CH) & (lax.rem(r, CH) == 0))
            def _():
                g = lax.div(r, CH)
                if stage == 0:
                    weight_term(g)
                    r_start(g, 0)
                elif stage == 1:
                    r_middle(g, 0)
                elif stage == 2:
                    r_last(g, 0)
                    r_start(g, 2)
                elif stage == 3:
                    r_middle(g, 1)
                else:
                    r_last(g, 1)

        for axis in range(5):

            @pl.when(i == K + 1 + 2 * axis)
            def _():
                if axis > 0:
                    skip_sum(axis - 1)
                if axis < 4:
                    for n in sk_range(axis):
                        sk_copy(axis, n).start()

        return carried

    def skip_sum(axis):
        total = sk[axis, 0]
        for n in sk_range(axis):
            sk_copy(axis, n).wait_recv()
            total = total + sk[axis, n]
        if axis < 3:
            sk[axis + 1, 0] = total
        else:
            dskip_ref[...] = total[0:1, :HEADS] * (1.0 / 32.0)

    def prepare(k):
        g = lax.div(k, CH)
        get_g(k).wait()
        xv = xs[k].astype(F32)
        gv = gs[k].astype(F32)
        scaled = (factor(0, k) * gv).astype(BF)
        gb[k, :128] = scaled[:HALF]
        gb[k, 384:512] = scaled[HALF:]
        gb[k, 128:256] = (dot(ft2[k].T.astype(BF), picks) * gv[HALF:]).astype(BF)
        product = jnp.sum(gv * xv, axis=0, keepdims=True)
        lane8 = lane[:8]
        tally = sk[0, 0]
        for j in range(CH):
            one = jnp.sum(product[:, j * 128 : (j + 1) * 128], axis=1, keepdims=True)
            tally = jnp.where(lane8 == CH * k + j, one, tally)
        sk[0, 0] = tally
        fresh = lax.rem(k, CH) == 0
        more = dot_nt(gb[k, :256], xb[k, :128])
        ds_acc[g, :256] = jnp.where(fresh, 0.0, ds_acc[g, :256]) + more
        more = dot_nt(scaled[HALF:], xb[k, 256:384])
        ds_acc[g, 256:] = jnp.where(fresh, 0.0, ds_acc[g, 256:]) + more

    def blocks_of(g):
        return (
            jnp.where(low, ds_acc[g, :128], 0.0),
            ds_acc[g, 128:256],
            jnp.where(low, ds_acc[g, 256:], 0.0),
        )

    def carry(f):
        g = lax.div(f, CH)
        fresh = lax.rem(f, CH) == 0
        ev = er[f].astype(F32)
        for n in range(2):
            scaled = (row_of(3 + n, f) * ev).astype(BF)
            xb[f, 128 + 256 * n : 256 + 256 * n] = scaled
            half = slice(n * HALF, (n + 1) * HALF)
            more = dot_nt(gb[f, 384 * n : 384 * n + 128], scaled)
            dc_acc[half] = jnp.where(fresh, 0.0, dc_acc[half]) + more

        @pl.when(lax.rem(f, CH) == CH - 1)
        def _():
            d00, d10, d11 = (d.astype(BF) for d in blocks_of(g))
            b0, b1 = b4[g, :HALF], b4[g, HALF:]
            cg[0, g, :HALF] = (dc_acc[:HALF] + dot(d00, b0)).astype(BF)
            cg[0, g, HALF:] = (dc_acc[HALF:] + dot(d10, b0) + dot(d11, b1)).astype(BF)
            cg_copy(g).start()

    def weight_term(g):
        cg_copy(g).wait_recv()
        mine = cg[0, g].astype(F32).T.astype(BF)
        other = cg[1, g].astype(F32).T.astype(BF)
        for n in range(16):
            part = slice(n * 256, (n + 1) * 256)
            term = dot(mine, li[0, :, part]) + dot(other, li[1, :, part])
            red[g, n // 4, n % 4] = term.astype(BF)

    def finish(k):
        g = lax.div(k, CH)
        lv = lr[k].astype(F32)
        fresh = lax.rem(k, CH) == 0
        for n, there in enumerate((256, 512)):
            scaled = (row_of(1 + n, k) * lv).astype(BF)
            gb[k, there : there + 128] = scaled
            half = slice(n * HALF, (n + 1) * HALF)
            more = dot_nt(xb[k, 256 * n : 256 * n + 128], scaled)
            db_acc[half] = jnp.where(fresh, 0.0, db_acc[half]) + more
        back = factor(1, k)
        gain = row_of(5, k)
        through = row_of(0, k) * jnp.sum(er[k].astype(F32) * lv, axis=0, keepdims=True)
        through = through + jnp.sum(own[k].astype(F32) * lv, axis=0, keepdims=True)
        heads = jnp.where(
            lax.broadcasted_iota(jnp.int32, (CW, 128), 1)
            == CH * k + lax.div(lax.broadcasted_iota(jnp.int32, (CW, 128), 0), 128),
            1.0,
            0.0,
        ).astype(BF)
        for n in range(2):
            half = slice(n * HALF, (n + 1) * HALF)
            if n == 0:
                dxs = dot(ls[g, :HALF], gb[k, :384])
                ys = dot(ly[g, :HALF], xb[k, :256])
                v = gb[k, :128].astype(F32) * ys - xb[k, :128].astype(F32) * dxs
            else:
                dxs = dot(ls[g, HALF:, :256], gb[k, 384:640])
                ys = dot(ly[g, HALF:], xb[k, 256:512])
                v = gb[k, 384:512].astype(F32) * ys - xb[k, 256:384].astype(F32) * dxs
                v = v + gb[k, 128:256].astype(F32) * dot(s10[g], xb[k, :128])
                v = v + jnp.where(row128 == HALF - 1, through, 0.0)
            gs[k, half] = (gain * gs[k, half].astype(F32) + back[half] * dxs).astype(BF)
            coarse = v.astype(BF)
            rest = (v - coarse.astype(F32)).astype(BF)
            acc[half] += dot(coarse, heads) + dot(rest, heads)
        put_x(k).start()
        @pl.when(lax.rem(k, CH) == CH - 1)
        def _():
            d00, d10, d11 = (d.T.astype(BF) for d in blocks_of(g))
            c0, c1 = cb[g, :HALF], cb[g, HALF:]
            there = pl.ds(pl.multiple_of(g * 128, 128), 128)
            db_ref[:HALF, there] = (db_acc[:HALF] + dot(d00, c0) + dot(d10, c1)).astype(BF)
            db_ref[HALF:, there] = (db_acc[HALF:] + dot(d11, c1)).astype(BF)

    lax.fori_loop(0, STEPS, step, 0)
    for n in range(1, 4):
        x_copy(n).start()
    turned_acc = acc[...].T
    dlog = jnp.dot(turned_acc, tri, precision=HIGHEST, preferred_element_type=F32)
    dlog_ref[...] = dlog[:HEADS]
    total = red[s, z, y].astype(F32)
    for n in range(1, 4):
        x_copy(n).wait_recv()
    for n in range(3):
        total = total + xr[n].astype(F32)
    fin[c, s] = total.astype(BF)
    for n, other in spread:
        a_copy(n, other).start()
    for n, other in spread:
        a_copy(n, other).wait_recv()

    def drain(k, carried):
        put_x(k).wait()

        @pl.when(s < 3)
        def _():
            fwd(k).wait_send()

        @pl.when(s > 0)
        def _():
            bwd(k).wait_send()

        return carried

    lax.fori_loop(0, K, drain, 0)

    def drain_groups(g, _):
        cg_copy(g).wait_send()
        for p in range(2):
            for stage in range(4):
                for d in range(2):
                    r_copy(g, p, stage, d).wait_send()
        return _

    lax.fori_loop(0, GROUPS, drain_groups, 0)
    for q in range(4):
        cp_copy(q).wait_send()
        for p in range(2):
            for stage in range(4):
                for d in range(2):
                    w_copy(q, p, stage, d).wait_send()
    for n in range(1, 4):
        x_copy(n).wait_send()
    for n, other in spread:
        a_copy(n, other).wait_send()
    for axis in range(4):
        for n in sk_range(axis):
            sk_copy(axis, n).wait_send()


def publish(
    dx_in, fin_in, db_in, dlog_in, dskip_in, dx_out, dw_out, db_out, dlog_out, dskip_out,
    dx_held, fin, db_held, dlog_held, dskip_held, came, left,
):
    rows = [pl.ds(n * 32, 32) for n in range(8)]
    moves = [(fin_in, fin, None)]
    moves += [(dx_in.at[r], dx_held.at[r], dx_out.at[r]) for r in rows]
    moves += [(db_in, db_held, db_out), (dlog_in, dlog_held, dlog_out)]
    moves += [(dskip_in, dskip_held, dskip_out)]
    loads = [pltpu.make_async_copy(m[0], m[1], came.at[n]) for n, m in enumerate(moves)]
    stores = [pltpu.make_async_copy(m[1], m[2], left.at[n]) for n, m in enumerate(moves) if n > 0]
    for copy in loads:
        copy.start()
    loads[0].wait()
    for load, store in zip(loads[1:], stores):
        load.wait()
        store.start()
    for h in range(2):
        for g in range(GROUPS):
            dw_out[h * 256 : (h + 1) * 256, g * 128 : (g + 1) * 128] = fin[h, g].astype(F32).T * (
                1.0 / 32.0
            )
    for copy in stores:
        copy.wait()


def on_device(layer_input, c_weight, head_input, b_input, log_decay, skip_gain, out_grad):
    vmem = pl.BlockSpec(memory_space=pltpu.VMEM)
    hbm = pl.BlockSpec(memory_space=pl.ANY)
    dma = pltpu.SemaphoreType.DMA

    def bf(*shape):
        return pltpu.VMEM(shape, BF)

    def f32(*shape):
        return pltpu.VMEM(shape, F32)

    chunked = (K, TOK, CW)
    states = (K, 128, CW)
    dx, db, fin, dlog, dskip = pl.pallas_call(
        kernel,
        out_shape=(
            jax.ShapeDtypeStruct((TOK, DIM), BF),
            jax.ShapeDtypeStruct((TOK, 512), BF),
            jax.ShapeDtypeStruct((2, GROUPS, 128, 256), BF),
            jax.ShapeDtypeStruct((HEADS, TOK), F32),
            jax.ShapeDtypeStruct((1, HEADS), F32),
        ),
        in_specs=[hbm, hbm, hbm, vmem, vmem, vmem, hbm],
        out_specs=(hbm, vmem, vmem, vmem, vmem),
        scratch_shapes=[
            bf(*chunked),
            bf(*chunked),
            bf(K, 640, CW),
            bf(K, 512, CW),
            bf(2, TOK, DIM // 2),
            bf(4, 4, 4, 256, 128),
            bf(*states),
            bf(*states),
            bf(*states),
            bf(*states),
            bf(*states),
            bf(GROUPS, 4, 4, 128, 256),
            bf(GROUPS, 2, 2, 4, 32, 256),
            bf(GROUPS, 2, 2, 4, 64, 256),
            bf(GROUPS, 2, 2, 32, 256),
            bf(GROUPS, 2, 2, 64, 256),
            f32(2, K, 2 * CH, TOK),
            f32(K, 2 * CH, HALF),
            f32(6, HEADS, 128),
            bf(GROUPS, TOK, 128),
            bf(GROUPS, 128, TOK),
            bf(GROUPS, TOK, 128),
            bf(GROUPS, 128, TOK),
            bf(GROUPS, TOK, 384),
            bf(GROUPS, TOK, 256),
            bf(GROUPS, HALF, HALF),
            f32(GROUPS, TOK, 128),
            f32(GROUPS, TOK, 128),
            f32(GROUPS, TOK, 128),
            f32(GROUPS, 384, HALF),
            f32(TOK, 128),
            f32(TOK, 128),
            bf(2, GROUPS, TOK, 128),
            f32(TOK, 128),
            bf(3, 128, 256),
            f32(4, 4, 8, 128),
            dma((K,)),
            dma((K,)),
            dma,
            dma((4,)),
            dma((K,)),
            dma,
            dma,
            dma((4, 2, 4, 2)),
            dma((4, 2, 4, 2)),
            dma((K,)),
            dma((K,)),
            dma((K,)),
            dma((K,)),
            dma((4,)),
            dma((4,)),
            dma((GROUPS,)),
            dma((GROUPS,)),
            dma((GROUPS, 2, 4, 2)),
            dma((GROUPS, 2, 4, 2)),
            dma((4,)),
            dma((4,)),
            dma((4, 2)),
            dma((4, 2)),
            dma((4, 4)),
            dma((4, 4)),
        ],
        compiler_params=pltpu.CompilerParams(
            collective_id=0, has_side_effects=True, vmem_limit_bytes=62 * 1024 * 1024
        ),
    )(
        layer_input[0],
        c_weight,
        head_input[0],
        b_input[0],
        log_decay[0],
        skip_gain[None],
        out_grad[0],
    )
    dx, dw, db, dlog, dskip = pl.pallas_call(
        publish,
        out_shape=(
            jax.ShapeDtypeStruct((TOK, DIM), BF),
            jax.ShapeDtypeStruct((512, 512), F32),
            jax.ShapeDtypeStruct((TOK, 512), BF),
            jax.ShapeDtypeStruct((HEADS, TOK), F32),
            jax.ShapeDtypeStruct((1, HEADS), F32),
        ),
        in_specs=[hbm] * 5,
        out_specs=(hbm, vmem, hbm, hbm, hbm),
        scratch_shapes=[
            bf(TOK, DIM),
            bf(2, GROUPS, 128, 256),
            bf(TOK, 512),
            f32(HEADS, TOK),
            f32(1, HEADS),
            dma((12,)),
            dma((12,)),
        ],
        compiler_params=pltpu.CompilerParams(vmem_limit_bytes=62 * 1024 * 1024),
    )(dx, fin, db, dlog, dskip)
    return dx[None], db[None], dw, dlog[None], dskip[0]


def solution(mesh):
    token = P(("fsdp", "dp"), "seq", None)
    decay = P(("fsdp", "dp"), None, "seq")
    rows = P("fsdp", None)
    return jax.shard_map(
        on_device,
        mesh=mesh,
        in_specs=(token, rows, token, token, decay, P(), token),
        out_specs=(token, token, rows, decay, P()),
        check_vma=False,
    )
```

```python
import jax
import jax.numpy as jnp
from jax import lax
from jax.experimental import pallas as pl
from jax.experimental.pallas import tpu as pltpu
from jax.sharding import PartitionSpec as P

HEADS = 64
GROUPS = 4
TOK = 256
HALF = 128
DIM = 8192
CH = 4
K = HEADS // CH
CW = CH * 128
AHEAD = 4
STEPS = 26
BF = jnp.bfloat16
F32 = jnp.float32
MESH = pl.DeviceIdType.MESH
HIGHEST = lax.Precision.HIGHEST
NT = (((1,), (1,)), ((), ()))


def dot(a, b):
    return jnp.dot(a, b, preferred_element_type=F32)


def dot_nt(a, b):
    return lax.dot_general(a, b, NT, preferred_element_type=F32)


def kernel(
    li_hbm,
    cw_hbm,
    x_hbm,
    b_ref,
    log_ref,
    skip_ref,
    g_hbm,
    dx_hbm,
    db_ref,
    fin,
    dlog_ref,
    dskip_ref,
    xs,
    gs,
    gb,
    xb,
    li,
    w,
    er,
    own,
    eout,
    lr,
    adj,
    red,
    t1,
    u1,
    t2,
    u2,
    ft,
    ft2,
    vals,
    b4,
    bt,
    cb,
    ct,
    ls,
    ly,
    s10,
    cp_own,
    cp_send,
    cp_recv,
    ds_acc,
    dc_acc,
    db_acc,
    cg,
    acc,
    xr,
    sk,
    load_x,
    load_g,
    load_li,
    load_w,
    store_x,
    li_send,
    li_recv,
    w_send,
    w_recv,
    f_send,
    f_recv,
    b_send,
    b_recv,
    cp_ssem,
    cp_rsem,
    cg_send,
    cg_recv,
    r_send,
    r_recv,
    x_send,
    x_recv,
    a_send,
    a_recv,
    sk_send,
    sk_recv,
):
    s = lax.axis_index("seq")
    fs = lax.axis_index("fsdp")
    c = lax.axis_index("dp")
    z, y = lax.div(fs, 4), lax.rem(fs, 4)

    def at(seq=None, zz=None, yy=None, core=None):
        seq = s if seq is None else seq
        zz = z if zz is None else zz
        yy = y if yy is None else yy
        core = c if core is None else core
        return {"seq": seq, "fsdp": zz * 4 + yy, "dp": core}

    def plus(i, n):
        return lax.rem(i + n, 4)

    def remote(src, dst, send, recv, device):
        return pltpu.make_async_remote_copy(
            src_ref=src,
            dst_ref=dst,
            send_sem=send,
            recv_sem=recv,
            device_id=device,
            device_id_type=MESH,
        )

    sibling = at(core=1 - c)

    def lanes(k):
        return pl.ds(pl.multiple_of(k * CW, CW), CW)

    def get_x(k):
        return pltpu.make_async_copy(x_hbm.at[:, lanes(k)], xs.at[k], load_x.at[k])

    def get_g(k):
        return pltpu.make_async_copy(g_hbm.at[:, lanes(k)], gs.at[k], load_g.at[k])

    def put_x(k):
        return pltpu.make_async_copy(gs.at[k], dx_hbm.at[:, lanes(k)], store_x)

    def get_w(q):
        return pltpu.make_async_copy(
            cw_hbm.at[pl.ds(pl.multiple_of(c * 256, 256), 256), pl.ds(q * 128, 128)],
            w.at[q, z, y],
            load_w.at[q],
        )

    def li_lanes(k, core):
        return pl.ds(pl.multiple_of(k * 512 + core * 256, 256), 256)

    def li_slot(slot, k):
        return li.at[slot, :, pl.ds(pl.multiple_of(k * 256, 256), 256)]

    def fwd(k):
        return remote(eout.at[k], er.at[k], f_send, f_recv.at[k], at(seq=plus(s, 1)))

    def bwd(k):
        return remote(adj.at[k], lr.at[k], b_send, b_recv.at[k], at(seq=plus(s, 3)))

    def toward(axis, d):
        if axis == 0:
            return at(zz=plus(z, 1 if d == 0 else 3))
        return at(yy=plus(y, 1 if d == 0 else 3))

    def w_copy(q, p, stage, d):
        phase, second = stage // 2, stage % 2
        axis = (1 - p) if phase == 0 else p
        me = z if axis == 0 else y
        idx = me if second == 0 else plus(me, 3 if d == 0 else 1)
        rows = pl.ds(p * 128, 128) if second == 0 else pl.ds(p * 128 + d * 64, 64)
        if phase == 0:
            ref = w.at[:, idx, y, rows] if axis == 0 else w.at[:, z, idx, rows]
        else:
            ref = w.at[q, idx, :, rows] if axis == 0 else w.at[q, :, idx, rows]
        return remote(ref, ref, w_send.at[stage], w_recv.at[q, stage], toward(axis, d))

    def w_start(q, stage):
        for p in range(2):
            for d in range(2):
                w_copy(q, p, stage, d).start()

    def w_wait(q, stage):
        ref = w.at[q, 0:2] if stage % 2 == 0 else w.at[q, 0]
        remote(ref, ref, w_send.at[stage], w_recv.at[q, stage], sibling).wait_recv()

    def w_sent(stage):
        ref = (w.at[0, 0:2], w.at[0, 0], w.at[0:2], w.at[0])[stage]
        remote(ref, ref, w_send.at[stage], w_recv.at[0, stage], sibling).wait_send()

    def cp_copy(q):
        return remote(cp_send.at[q], cp_recv.at[q], cp_ssem, cp_rsem.at[q], sibling)

    def cg_copy(g):
        return remote(cg.at[0, g], cg.at[1, g], cg_send, cg_recv.at[g], sibling)

    def r_axis(p, phase):
        return p if phase == 0 else 1 - p

    def r_ref(g, p, phase, idx, rows):
        if phase == 0:
            return red.at[g, idx, :, rows] if p == 0 else red.at[g, :, idx, rows]
        return red.at[g, z, idx, rows] if p == 0 else red.at[g, idx, y, rows]

    def r_full(p):
        return pl.ds(p * 64, 64)

    def r_half(p, h):
        return pl.ds(p * 64 + h * 32, 32)

    def r_copy(g, p, stage, d):
        phase, second = stage // 2, stage % 2
        axis = r_axis(p, phase)
        me = z if axis == 0 else y
        if second == 0:
            src = r_ref(g, p, phase, plus(me, 2), r_half(p, d))
            dst = (t1 if phase == 0 else t2).at[g, p, d]
        else:
            src = r_ref(g, p, phase, plus(me, 1 if d == 0 else 3), r_full(p))
            dst = (u1 if phase == 0 else u2).at[g, p, d]
        return remote(src, dst, r_send.at[stage], r_recv.at[g, stage], toward(axis, d))

    def r_wait(g, stage):
        ref = (t1, u1, t2, u2)[stage].at[g]
        remote(ref, ref, r_send.at[stage], r_recv.at[g, stage], sibling).wait_recv()

    def r_sent(stage):
        ref = (t1, u1, t2, u2)[stage]
        remote(ref, ref, r_send.at[stage], r_recv.at[0, stage], sibling).wait_send()

    def r_start(g, stage):
        for p in range(2):
            for d in range(2):
                r_copy(g, p, stage, d).start()

    def r_middle(g, phase):
        r_wait(g, 2 * phase)
        for p in range(2):
            me = z if r_axis(p, phase) == 0 else y
            for d in range(2):
                ref = r_ref(g, p, phase, plus(me, 1 if d == 0 else 3), r_half(p, d))
                got = (t1 if phase == 0 else t2)[g, p, d]
                ref[...] = (ref[...].astype(F32) + got.astype(F32)).astype(BF)
                r_copy(g, p, 2 * phase + 1, d).start()

    def r_last(g, phase):
        r_wait(g, 2 * phase + 1)
        for p in range(2):
            me = z if r_axis(p, phase) == 0 else y
            buf = u1 if phase == 0 else u2
            ref = r_ref(g, p, phase, me, r_full(p))
            total = ref[...].astype(F32) + buf[g, p, 0].astype(F32) + buf[g, p, 1].astype(F32)
            ref[...] = total.astype(BF)

    def x_copy(n):
        to = plus(s, n)
        return remote(red.at[to, z, y], xr.at[n - 1], x_send, x_recv, at(seq=to))

    def a_copy(n, other):
        to = at(seq=plus(s, n), core=1 - c if other else c)
        return remote(fin.at[c, s], fin.at[c, s], a_send.at[other], a_recv.at[other], to)

    spread = [(n, other) for other in range(2) for n in range(4)][1:]

    def sk_copy(axis, n):
        if axis == 3:
            return remote(sk.at[3, 0], sk.at[3, 1], sk_send.at[3], sk_recv.at[3], sibling)
        to = (
            at(zz=plus(z, n))
            if axis == 0
            else (at(yy=plus(y, n)) if axis == 1 else at(seq=plus(s, n)))
        )
        return remote(sk.at[axis, 0], sk.at[axis, n], sk_send.at[axis], sk_recv.at[axis], to)

    def sk_all(axis):
        ref = sk.at[3, 1] if axis == 3 else sk.at[axis, 1:4]
        return remote(ref, ref, sk_send.at[axis], sk_recv.at[axis], sibling)

    def a_all(other):
        ref = fin.at[0] if other else fin.at[0, 0:3]
        return remote(ref, ref, a_send.at[other], a_recv.at[other], sibling)

    def x_all():
        return remote(xr, xr, x_send, x_recv, sibling)

    def sk_range(axis):
        return range(1, 2) if axis == 3 else range(1, 4)

    for q in range(4):
        get_w(q).start()

    def load(k, carried):
        get_x(k).start()
        return carried

    lax.fori_loop(0, K, load, 0)

    barrier = pltpu.get_barrier_semaphore()
    peers = [sibling]
    for n in range(1, 4):
        peers += [at(seq=plus(s, n)), at(zz=plus(z, n)), at(yy=plus(y, n))]
        peers += [at(seq=plus(s, n), core=1 - c)]
    for peer in peers:
        pl.semaphore_signal(barrier, inc=1, device_id=peer, device_id_type=MESH)

    def load_more(k, carried):
        get_g(k).start()
        return carried

    lax.fori_loop(0, K, load_more, 0)

    rows_i = lax.broadcasted_iota(jnp.int32, (TOK, TOK), 0)
    cols_i = lax.broadcasted_iota(jnp.int32, (TOK, TOK), 1)
    tri = jnp.where(cols_i <= rows_i, 1.0, 0.0).astype(F32)
    low = rows_i[:HALF, :HALF] >= cols_i[:HALF, :HALF]
    high = rows_i[:HALF, :HALF] <= cols_i[:HALF, :HALF]
    lane = lax.broadcasted_iota(jnp.int32, (TOK, 128), 1)
    row = lax.broadcasted_iota(jnp.int32, (TOK, 128), 0)
    row128 = lax.broadcasted_iota(jnp.int32, (HALF, 1), 0)
    picks = jnp.where(
        lax.rem(lax.broadcasted_iota(jnp.int32, (2 * CH, CW), 0), CH)
        == lax.div(lax.broadcasted_iota(jnp.int32, (2 * CH, CW), 1), 128),
        1.0,
        0.0,
    ).astype(BF)

    running = lax.dot_general(log_ref[...], tri, NT, precision=HIGHEST, preferred_element_type=F32)
    ending = running[:, TOK - 1 : TOK]
    mid0 = running[:, HALF // 2 - 1 : HALF // 2]
    mid1 = running[:, HALF + HALF // 2 - 1 : HALF + HALF // 2]
    for n, value in enumerate((ending, ending - mid0, ending - mid1, mid0, mid1)):
        vals[n] = jnp.broadcast_to(jnp.exp(value), (HEADS, 128))
    gain = jnp.concatenate([skip_ref[...]] * 2, axis=1)
    gains = jnp.where(lane[:HEADS] == row[:HEADS], gain, 0.0)
    vals[5] = jnp.broadcast_to(jnp.sum(gains, axis=1, keepdims=True), (HEADS, 128))
    middle = jnp.where(cols_i[:HEADS] < HALF, mid0, mid1)

    def split(values):
        coarse = values.astype(BF).astype(F32)
        return coarse, (values - coarse).astype(BF).astype(F32)

    for n, values in enumerate((running - middle, middle - running)):
        for half, part in enumerate(split(jnp.exp(values))):
            for k in range(K):
                ft[n, k, half * CH : (half + 1) * CH] = part[k * CH : (k + 1) * CH]
    for half, part in enumerate(split(jnp.exp(running[:, HALF:] - mid0))):
        for k in range(K):
            ft2[k, half * CH : (half + 1) * CH] = part[k * CH : (k + 1) * CH]
    acc[...] = jnp.zeros_like(acc)
    sk[0, 0] = jnp.zeros((8, 128), F32)

    def factor(n, k):
        return dot(ft[n, k].T.astype(BF), picks)

    def row_of(n, k):
        return jnp.concatenate([vals[n, pl.ds(CH * k + j, 1), :] for j in range(CH)], axis=1)

    for g in range(GROUPS):
        part = b_ref[:, g * 128 : (g + 1) * 128]
        b4[g] = part
        bt[g] = part.astype(F32).T.astype(BF)
        ls[g, :HALF, 256:] = part[:HALF]
        ls[g, HALF:, 128:256] = part[HALF:]

    @pl.when(s == 0)
    def _():
        er[...] = jnp.zeros_like(er)

    @pl.when(s == 3)
    def _():
        lr[...] = jnp.zeros_like(lr)
        own[...] = jnp.zeros_like(own)

    def first(k):
        g = lax.div(k, CH)
        get_x(k).wait()
        scaled = (factor(1, k) * xs[k].astype(F32)).astype(BF)
        xb[k, :128] = scaled[:HALF]
        xb[k, 256:384] = scaled[HALF:]

        @pl.when(s < 3)
        def _():
            state = row_of(1, k) * dot(bt[g, :, :HALF], scaled[:HALF])
            state = (state + row_of(2, k) * dot(bt[g, :, HALF:], scaled[HALF:])).astype(BF)
            own[k] = state

            @pl.when(s == 0)
            def _():
                eout[k] = state
                fwd(k).start()

    pl.semaphore_wait(barrier, len(peers))
    for q in range(4):
        get_w(q).wait()
    w_start(0, 0)

    def load_part(k, carried):
        pltpu.make_async_copy(li_hbm.at[:, li_lanes(k, c)], li_slot(0, k), load_li).start()
        remote(li_hbm.at[:, li_lanes(k, 1 - c)], li_slot(1, k), li_send, li_recv, sibling).start()
        return carried

    lax.fori_loop(0, 16, load_part, 0)

    def first_of(k, carried):
        first(k)
        return carried

    lax.fori_loop(0, AHEAD, first_of, 0)
    w_wait(0, 0)
    w_start(0, 1)
    w_wait(0, 1)
    w_start(0, 2)

    pairs = lax.div(s * (s - 1), 2)
    triples = lax.div(s * (s - 1) * (s - 2), 6)
    slot_a = 1 + 2 * s - 3 * pairs + 2 * triples
    slot_b = 3 + 2 * s - 3 * pairs + triples
    slot_c = 5 + s - pairs - 3 * triples
    slot_d = slot_c + 2
    slot_e = slot_c + 4
    trail = 9 - s - pairs - triples

    def project(q):
        weights = w[q].reshape(DIM // 2, 128)
        cp_send[q] = dot(li[1], weights)
        cp_copy(q).start()
        cp_own[q] = dot(li[0], weights)

    def projected(g):
        cp_copy(g).wait_recv()
        mine = (cp_own[g] + cp_recv[g]).astype(BF)
        cb[g] = mine
        ct[g] = mine.astype(F32).T.astype(BF)
        scores = dot_nt(mine, b4[g])
        flipped = dot_nt(b4[g], mine)
        ly[g, :HALF, :128] = jnp.where(low, scores[:HALF, :HALF], 0.0).astype(BF)
        ly[g, HALF:, :128] = jnp.where(low, scores[HALF:, HALF:], 0.0).astype(BF)
        ly[g, :, 128:] = mine
        s10[g] = scores[HALF:, :HALF].astype(BF)
        ls[g, :HALF, :128] = jnp.where(high, flipped[:HALF, :HALF], 0.0).astype(BF)
        ls[g, :HALF, 128:256] = flipped[:HALF, HALF:].astype(BF)
        ls[g, HALF:, :128] = jnp.where(high, flipped[HALF:, HALF:], 0.0).astype(BF)

    def step(i, carried):
        f = i - s

        @pl.when((f >= 0) & (f < K) & (s > 0))
        def _():
            fwd(f).wait_recv()

            @pl.when(s < 3)
            def _():
                rounded = row_of(0, f).astype(BF).astype(F32)
                eout[f] = (rounded * er[f].astype(F32) + own[f].astype(F32)).astype(BF)
                fwd(f).start()

        @pl.when(i + AHEAD < K)
        def _():
            first(i + AHEAD)

        for g, slot in enumerate((slot_b, slot_c, slot_d, slot_e)):

            @pl.when(i == slot + 1)
            def _():
                projected(g)

        b = i - trail

        @pl.when((b >= 0) & (b < K))
        def _():
            bg = lax.div(b, CH)

            @pl.when(s > 0)
            def _():
                term = row_of(3, b) * dot(ct[bg, :, :HALF], gb[b, :128])
                term = term + row_of(4, b) * dot(ct[bg, :, HALF:], gb[b, 384:512])
                adj[b] = term.astype(BF)

            @pl.when(s < 3)
            def _():
                bwd(b).wait_recv()

                @pl.when(s > 0)
                def _():
                    rounded = row_of(0, b).astype(BF).astype(F32)
                    adj[b] = (rounded * lr[b].astype(F32) + adj[b].astype(F32)).astype(BF)

            @pl.when(s > 0)
            def _():
                bwd(b).start()

        @pl.when(i == slot_a)
        def _():
            w_wait(0, 2)
            w_start(0, 3)
            w_start(1, 2)

        @pl.when(i == slot_b)
        def _():
            pltpu.make_async_copy(li.at[0], li.at[0], load_li).wait()
            remote(li.at[1], li.at[1], li_send, li_recv, sibling).wait()
            w_wait(0, 3)
            project(0)
            w_wait(1, 2)
            w_start(1, 3)
            w_start(2, 2)

        @pl.when(i == slot_c)
        def _():
            w_wait(1, 3)
            project(1)
            w_wait(2, 2)
            w_start(2, 3)
            w_start(3, 2)

        @pl.when(i == slot_d)
        def _():
            w_wait(2, 3)
            project(2)
            w_wait(3, 2)
            w_start(3, 3)

        @pl.when(i == slot_e)
        def _():
            w_wait(3, 3)
            project(3)

        @pl.when(i < K)
        def _():
            prepare(i)

        @pl.when((f >= 0) & (f < K))
        def _():
            carry(f)

        @pl.when((b >= 1) & (b <= K))
        def _():
            finish(b - 1)

        for stage, after in enumerate((0, 2, 4, 5, 6)):
            r = f - CH - after

            @pl.when((r >= 0) & (r < GROUPS * CH) & (lax.rem(r, CH) == 0))
            def _():
                g = lax.div(r, CH)
                if stage == 0:
                    weight_term(g)
                    r_start(g, 0)
                elif stage == 1:
                    r_middle(g, 0)
                elif stage == 2:
                    r_last(g, 0)
                    r_start(g, 2)
                elif stage == 3:
                    r_middle(g, 1)
                else:
                    r_last(g, 1)

        for axis in range(5):

            @pl.when(i == K + 1 + 2 * axis)
            def _():
                if axis > 0:
                    skip_sum(axis - 1)
                if axis < 4:
                    for n in sk_range(axis):
                        sk_copy(axis, n).start()

        return carried

    def skip_sum(axis):
        sk_all(axis).wait_recv()
        total = sk[axis, 0]
        for n in sk_range(axis):
            total = total + sk[axis, n]
        if axis < 3:
            sk[axis + 1, 0] = total
        else:
            dskip_ref[...] = total[0:1, :HEADS] * (1.0 / 32.0)

    def prepare(k):
        g = lax.div(k, CH)
        get_g(k).wait()
        xv = xs[k].astype(F32)
        gv = gs[k].astype(F32)
        scaled = (factor(0, k) * gv).astype(BF)
        gb[k, :128] = scaled[:HALF]
        gb[k, 384:512] = scaled[HALF:]
        gb[k, 128:256] = (dot(ft2[k].T.astype(BF), picks) * gv[HALF:]).astype(BF)
        product = jnp.sum(gv * xv, axis=0, keepdims=True)
        lane8 = lane[:8]
        tally = sk[0, 0]
        for j in range(CH):
            one = jnp.sum(product[:, j * 128 : (j + 1) * 128], axis=1, keepdims=True)
            tally = jnp.where(lane8 == CH * k + j, one, tally)
        sk[0, 0] = tally
        fresh = lax.rem(k, CH) == 0
        more = dot_nt(gb[k, :256], xb[k, :128])
        ds_acc[g, :256] = jnp.where(fresh, 0.0, ds_acc[g, :256]) + more
        more = dot_nt(scaled[HALF:], xb[k, 256:384])
        ds_acc[g, 256:] = jnp.where(fresh, 0.0, ds_acc[g, 256:]) + more

    def blocks_of(g):
        return (
            jnp.where(low, ds_acc[g, :128], 0.0),
            ds_acc[g, 128:256],
            jnp.where(low, ds_acc[g, 256:], 0.0),
        )

    def carry(f):
        g = lax.div(f, CH)
        fresh = lax.rem(f, CH) == 0
        ev = er[f].astype(F32)
        for n in range(2):
            scaled = (row_of(3 + n, f) * ev).astype(BF)
            xb[f, 128 + 256 * n : 256 + 256 * n] = scaled
            half = slice(n * HALF, (n + 1) * HALF)
            more = dot_nt(gb[f, 384 * n : 384 * n + 128], scaled)
            dc_acc[half] = jnp.where(fresh, 0.0, dc_acc[half]) + more

        @pl.when(lax.rem(f, CH) == CH - 1)
        def _():
            d00, d10, d11 = (d.astype(BF) for d in blocks_of(g))
            b0, b1 = b4[g, :HALF], b4[g, HALF:]
            cg[0, g, :HALF] = (dc_acc[:HALF] + dot(d00, b0)).astype(BF)
            cg[0, g, HALF:] = (dc_acc[HALF:] + dot(d10, b0) + dot(d11, b1)).astype(BF)
            cg_copy(g).start()

    def weight_term(g):
        cg_copy(g).wait_recv()
        mine = cg[0, g].astype(F32).T.astype(BF)
        other = cg[1, g].astype(F32).T.astype(BF)
        for n in range(16):
            part = slice(n * 256, (n + 1) * 256)
            term = dot(mine, li[0, :, part]) + dot(other, li[1, :, part])
            red[g, n // 4, n % 4] = term.astype(BF)

    def finish(k):
        g = lax.div(k, CH)
        lv = lr[k].astype(F32)
        fresh = lax.rem(k, CH) == 0
        for n, there in enumerate((256, 512)):
            scaled = (row_of(1 + n, k) * lv).astype(BF)
            gb[k, there : there + 128] = scaled
            half = slice(n * HALF, (n + 1) * HALF)
            more = dot_nt(xb[k, 256 * n : 256 * n + 128], scaled)
            db_acc[half] = jnp.where(fresh, 0.0, db_acc[half]) + more
        back = factor(1, k)
        gain = row_of(5, k)
        through = row_of(0, k) * jnp.sum(er[k].astype(F32) * lv, axis=0, keepdims=True)
        through = through + jnp.sum(own[k].astype(F32) * lv, axis=0, keepdims=True)
        heads = jnp.where(
            lax.broadcasted_iota(jnp.int32, (CW, 128), 1)
            == CH * k + lax.div(lax.broadcasted_iota(jnp.int32, (CW, 128), 0), 128),
            1.0,
            0.0,
        ).astype(BF)
        for n in range(2):
            half = slice(n * HALF, (n + 1) * HALF)
            if n == 0:
                dxs = dot(ls[g, :HALF], gb[k, :384])
                ys = dot(ly[g, :HALF], xb[k, :256])
                v = gb[k, :128].astype(F32) * ys - xb[k, :128].astype(F32) * dxs
            else:
                dxs = dot(ls[g, HALF:, :256], gb[k, 384:640])
                ys = dot(ly[g, HALF:], xb[k, 256:512])
                v = gb[k, 384:512].astype(F32) * ys - xb[k, 256:384].astype(F32) * dxs
                v = v + gb[k, 128:256].astype(F32) * dot(s10[g], xb[k, :128])
                v = v + jnp.where(row128 == HALF - 1, through, 0.0)
            gs[k, half] = (gain * gs[k, half].astype(F32) + back[half] * dxs).astype(BF)
            coarse = v.astype(BF)
            rest = (v - coarse.astype(F32)).astype(BF)
            acc[half] += dot(coarse, heads) + dot(rest, heads)
        put_x(k).start()
        @pl.when(lax.rem(k, CH) == CH - 1)
        def _():
            d00, d10, d11 = (d.T.astype(BF) for d in blocks_of(g))
            c0, c1 = cb[g, :HALF], cb[g, HALF:]
            there = pl.ds(pl.multiple_of(g * 128, 128), 128)
            db_ref[:HALF, there] = (db_acc[:HALF] + dot(d00, c0) + dot(d10, c1)).astype(BF)
            db_ref[HALF:, there] = (db_acc[HALF:] + dot(d11, c1)).astype(BF)

    lax.fori_loop(0, STEPS, step, 0)
    for n in range(1, 4):
        x_copy(n).start()
    turned_acc = acc[...].T
    dlog = jnp.dot(turned_acc, tri, precision=HIGHEST, preferred_element_type=F32)
    dlog_ref[...] = dlog[:HEADS]
    total = red[s, z, y].astype(F32)
    x_all().wait_recv()
    for n in range(3):
        total = total + xr[n].astype(F32)
    fin[c, s] = total.astype(BF)
    for n, other in spread:
        a_copy(n, other).start()
    a_all(0).wait_recv()
    a_all(1).wait_recv()

    pltpu.make_async_copy(gs, gs, store_x).wait()

    @pl.when(s < 3)
    def _():
        remote(eout, er, f_send, f_recv.at[0], sibling).wait_send()

    @pl.when(s > 0)
    def _():
        remote(adj, lr, b_send, b_recv.at[0], sibling).wait_send()

    for stage in range(4):
        w_sent(stage)
        r_sent(stage)
    remote(cp_send, cp_recv, cp_ssem, cp_rsem.at[0], sibling).wait_send()
    remote(cg.at[0], cg.at[1], cg_send, cg_recv.at[0], sibling).wait_send()
    x_all().wait_send()
    a_all(0).wait_send()
    a_all(1).wait_send()
    for axis in range(4):
        sk_all(axis).wait_send()


def publish(
    dx_in, fin_in, db_in, dlog_in, dskip_in, dx_out, dw_out, db_out, dlog_out, dskip_out,
    dx_held, fin, db_held, dlog_held, dskip_held, came, left,
):
    rows = [pl.ds(n * 32, 32) for n in range(8)]
    moves = [(fin_in, fin, None)]
    moves += [(dx_in.at[r], dx_held.at[r], dx_out.at[r]) for r in rows]
    moves += [(db_in, db_held, db_out), (dlog_in, dlog_held, dlog_out)]
    moves += [(dskip_in, dskip_held, dskip_out)]
    loads = [pltpu.make_async_copy(m[0], m[1], came.at[n]) for n, m in enumerate(moves)]
    stores = [pltpu.make_async_copy(m[1], m[2], left.at[n]) for n, m in enumerate(moves) if n > 0]
    for copy in loads:
        copy.start()
    loads[0].wait()
    for load, store in zip(loads[1:], stores):
        load.wait()
        store.start()
    for h in range(2):
        for g in range(GROUPS):
            dw_out[h * 256 : (h + 1) * 256, g * 128 : (g + 1) * 128] = fin[h, g].astype(F32).T * (
                1.0 / 32.0
            )
    for copy in stores:
        copy.wait()


def on_device(layer_input, c_weight, head_input, b_input, log_decay, skip_gain, out_grad):
    vmem = pl.BlockSpec(memory_space=pltpu.VMEM)
    hbm = pl.BlockSpec(memory_space=pl.ANY)
    dma = pltpu.SemaphoreType.DMA

    def bf(*shape):
        return pltpu.VMEM(shape, BF)

    def f32(*shape):
        return pltpu.VMEM(shape, F32)

    chunked = (K, TOK, CW)
    states = (K, 128, CW)
    dx, db, fin, dlog, dskip = pl.pallas_call(
        kernel,
        out_shape=(
            jax.ShapeDtypeStruct((TOK, DIM), BF),
            jax.ShapeDtypeStruct((TOK, 512), BF),
            jax.ShapeDtypeStruct((2, GROUPS, 128, 256), BF),
            jax.ShapeDtypeStruct((HEADS, TOK), F32),
            jax.ShapeDtypeStruct((1, HEADS), F32),
        ),
        in_specs=[hbm, hbm, hbm, vmem, vmem, vmem, hbm],
        out_specs=(hbm, vmem, vmem, vmem, vmem),
        scratch_shapes=[
            bf(*chunked),
            bf(*chunked),
            bf(K, 640, CW),
            bf(K, 512, CW),
            bf(2, TOK, DIM // 2),
            bf(4, 4, 4, 256, 128),
            bf(*states),
            bf(*states),
            bf(*states),
            bf(*states),
            bf(*states),
            bf(GROUPS, 4, 4, 128, 256),
            bf(GROUPS, 2, 2, 4, 32, 256),
            bf(GROUPS, 2, 2, 4, 64, 256),
            bf(GROUPS, 2, 2, 32, 256),
            bf(GROUPS, 2, 2, 64, 256),
            f32(2, K, 2 * CH, TOK),
            f32(K, 2 * CH, HALF),
            f32(6, HEADS, 128),
            bf(GROUPS, TOK, 128),
            bf(GROUPS, 128, TOK),
            bf(GROUPS, TOK, 128),
            bf(GROUPS, 128, TOK),
            bf(GROUPS, TOK, 384),
            bf(GROUPS, TOK, 256),
            bf(GROUPS, HALF, HALF),
            f32(GROUPS, TOK, 128),
            f32(GROUPS, TOK, 128),
            f32(GROUPS, TOK, 128),
            f32(GROUPS, 384, HALF),
            f32(TOK, 128),
            f32(TOK, 128),
            bf(2, GROUPS, TOK, 128),
            f32(TOK, 128),
            bf(3, 128, 256),
            f32(4, 4, 8, 128),
            dma((K,)),
            dma((K,)),
            dma,
            dma((4,)),
            dma,
            dma,
            dma,
            dma((4,)),
            dma((4, 4)),
            dma,
            dma((K,)),
            dma,
            dma((K,)),
            dma,
            dma((4,)),
            dma,
            dma((GROUPS,)),
            dma((4,)),
            dma((GROUPS, 4)),
            dma,
            dma,
            dma((2,)),
            dma((2,)),
            dma((4,)),
            dma((4,)),
        ],
        compiler_params=pltpu.CompilerParams(
            collective_id=0, has_side_effects=True, vmem_limit_bytes=62 * 1024 * 1024
        ),
    )(
        layer_input[0],
        c_weight,
        head_input[0],
        b_input[0],
        log_decay[0],
        skip_gain[None],
        out_grad[0],
    )
    dx, dw, db, dlog, dskip = pl.pallas_call(
        publish,
        out_shape=(
            jax.ShapeDtypeStruct((TOK, DIM), BF),
            jax.ShapeDtypeStruct((512, 512), F32),
            jax.ShapeDtypeStruct((TOK, 512), BF),
            jax.ShapeDtypeStruct((HEADS, TOK), F32),
            jax.ShapeDtypeStruct((1, HEADS), F32),
        ),
        in_specs=[hbm] * 5,
        out_specs=(hbm, vmem, hbm, hbm, hbm),
        scratch_shapes=[
            bf(TOK, DIM),
            bf(2, GROUPS, 128, 256),
            bf(TOK, 512),
            f32(HEADS, TOK),
            f32(1, HEADS),
            dma((12,)),
            dma((12,)),
        ],
        compiler_params=pltpu.CompilerParams(vmem_limit_bytes=62 * 1024 * 1024),
    )(dx, fin, db, dlog, dskip)
    return dx[None], db[None], dw, dlog[None], dskip[0]


def solution(mesh):
    token = P(("fsdp", "dp"), "seq", None)
    decay = P(("fsdp", "dp"), None, "seq")
    rows = P("fsdp", None)
    return jax.shard_map(
        on_device,
        mesh=mesh,
        in_specs=(token, rows, token, token, decay, P(), token),
        out_specs=(token, token, rows, decay, P()),
        check_vma=False,
    )
```
